256 devices in a mesh: tile: 8 (over z), dp: 32 (over x, y, core).
Axes of the slice: x: 4, y: 4, z: 8, core: 2. Of those that a mesh axis runs over, the one named last changes fastest.
Arguments:
- inputs: bfloat16 [32, 64, 288, 256], P('dp', 'tile'), may hold values from -6 to 6
- pre_first: bfloat16 [32, 64, 288, 256], P('dp', 'tile'), may hold values from -6 to 6
- pre_second: bfloat16 [32, 64, 288, 256], P('dp', 'tile'), may hold values from -6 to 6
- labels: int32 [32, 64, 288], P('dp', 'tile'), may hold values from 0 to 2
- classifier: bfloat16 [256, 3], replicated, may hold values from -0.375 to 0.375
- w_first: float32 [589824], P(('tile', 'dp')), may hold values from -0.125 to 0.125
- m_first: float32 [589824], P(('tile', 'dp')), may hold values from -48 to 48
- v_first: float32 [589824], P(('tile', 'dp')), may hold values from 0.589824 to 5.89824
- w_second: float32 [589824], P(('tile', 'dp')), may hold values from -0.125 to 0.125
- m_second: float32 [589824], P(('tile', 'dp')), may hold values from -48 to 48
- v_second: float32 [589824], P(('tile', 'dp')), may hold values from 0.589824 to 5.89824
Outputs:
- w_first_new: float32 [589824], P(('tile', 'dp'))
- m_first_new: float32 [589824], P(('tile', 'dp'))
- v_first_new: float32 [589824], P(('tile', 'dp'))
- w_second_new: float32 [589824], P(('tile', 'dp'))
- m_second_new: float32 [589824], P(('tile', 'dp'))
- v_second_new: float32 [589824], P(('tile', 'dp'))
- w_first_step: float32 [589824], P(('tile', 'dp'))
- w_second_step: float32 [589824], P(('tile', 'dp'))
The draws below stay inside these ranges and needn't reach their ends.
All inputs are finite; a program needn't handle non-finite values.
Results may differ from the reference program's by a relative error of at most 0.0017.
Values may be sent and summed in bfloat16 or wider, within the bound.
A program may use at most 64 MiB of HBM per device.

```python
import math
import jax
import jax.numpy as jnp
from jax import lax

CH = 256
CLASSES = 3
COLS = 288
STEP = 10
ROWS = 64
BATCH = 32
PIX_ALL = 589824
FLAT = 589824


def plant(values, stream_key, smallest, top_value):
    longest = values.shape.index(max(values.shape))
    spots = []
    for shift in (0, 1):
        where = [jax.random.randint(jax.random.fold_in(stream_key, axis), (), 0, length) for axis, length in enumerate(values.shape)]
        where[longest] = (where[longest] + shift) % values.shape[longest]
        spots.append(tuple(where))
    return values.at[spots[0]].set(smallest).at[spots[1]].set(top_value)


def shard_levels(rng, extent, cuts, smallest, high):
    level, own = 1.0, jax.random.fold_in(rng, 6)
    for position, shards_of in cuts:
        steps = jnp.exp(jax.random.uniform(jax.random.fold_in(own, position), (shards_of,), jnp.float32, smallest / len(cuts), high / len(cuts)))
        level = level * jnp.repeat(steps, extent[position] // shards_of).reshape([-1 if axis == position else 1 for axis in range(len(extent))])
    return level


def noise(rng, dims, scale, limit, cuts=(), held_as=jnp.bfloat16):
    values = scale * jax.random.normal(rng, dims, jnp.float32)
    if cuts:
        values = values * shard_levels(rng, dims, cuts, -0.22, 0.18)
    return jnp.clip(values, -limit, limit).astype(held_as)


def setup_inputs(seed: int = 0) -> dict:
    key_list = jax.random.split(jax.random.key(seed), 12)
    return {
        "inputs": noise(key_list[0], (BATCH, ROWS, COLS, CH), 1.0, 6.0, ((0, 32), (1, 8))),
        "pre_first": noise(key_list[1], (BATCH, ROWS, COLS, CH), 1.0, 6.0, ((0, 32), (1, 8))),
        "pre_second": noise(key_list[2], (BATCH, ROWS, COLS, CH), 1.0, 6.0, ((0, 32), (1, 8))),
        "labels": plant(jax.random.randint(key_list[3], (BATCH, ROWS, COLS), 0, 3), jax.random.fold_in(key_list[3], 1), 0, 2).astype(jnp.int32),
        "classifier": noise(key_list[4], (CH, CLASSES), CH ** -0.5, 0.375),
        "w_first": noise(key_list[5], (FLAT,), (9 * CH) ** -0.5, 0.125, ((0, 256),), jnp.float32),
        "m_first": noise(key_list[6], (FLAT,), (0.01 * PIX_ALL ** 0.5), 48.0, ((0, 256),), jnp.float32),
        "v_first": jnp.clip(jnp.exp(math.log(5.89824) - 2.3025851 * jax.random.uniform(key_list[7], (FLAT,), jnp.float32) ** shard_levels(key_list[7], (FLAT,), ((0, 256),), -0.2, 0.2)), 0.589824, 5.89824),
        "w_second": noise(key_list[8], (FLAT,), (9 * CH) ** -0.5, 0.125, ((0, 256),), jnp.float32),
        "m_second": noise(key_list[9], (FLAT,), (0.01 * PIX_ALL ** 0.5), 48.0, ((0, 256),), jnp.float32),
        "v_second": jnp.clip(jnp.exp(math.log(5.89824) - 2.3025851 * jax.random.uniform(key_list[10], (FLAT,), jnp.float32) ** shard_levels(key_list[10], (FLAT,), ((0, 256),), -0.2, 0.2)), 0.589824, 5.89824),
    }


beta_one = 0.9
beta_two = 0.999
epsilon = 1e-06
weight_decay = 0.01
learn_rate = 0.002

def pad_image(field):
    return jnp.pad(field, ((1, 1), (1, 1), (0, 0)))

def weight_terms(padded, grad):
    height, width, chans = grad.shape
    flat_grad = grad.reshape(-1, chans)
    terms = []
    for row_off in range(3):
        for col_off in range(3):
            window = padded[row_off:row_off + height, col_off:col_off + width].reshape(-1, chans)
            terms.append(jnp.dot(window.T, flat_grad, preferred_element_type=jnp.float32))
    return jnp.stack(terms).reshape(-1)

def input_terms(padded, kernel):
    height = padded.shape[0] - 2
    width = padded.shape[1] - 2
    chans = padded.shape[2]
    total = jnp.zeros((height * width, chans), jnp.float32)
    for row_off in range(3):
        for col_off in range(3):
            window = padded[2 - row_off:2 - row_off + height, 2 - col_off:2 - col_off + width].reshape(-1, chans)
            total = total + jnp.dot(window, kernel[row_off, col_off].T, preferred_element_type=jnp.float32)
    return total.reshape(height, width, chans)

def lamb_step(grad, weight, first, second):
    first_new = beta_one * first + (1.0 - beta_one) * grad
    second_new = beta_two * second + (1.0 - beta_two) * grad * grad
    corr_one = 1.0 - beta_one ** STEP
    corr_two = 1.0 - beta_two ** STEP
    update = first_new / corr_one / (jnp.sqrt(second_new / corr_two) + epsilon) + weight_decay * weight
    trust = jnp.sqrt(jnp.sum(weight * weight)) / jnp.sqrt(jnp.sum(update * update))
    scaled = trust * update
    return (weight - learn_rate * scaled, first_new, second_new, scaled)

def reference(inputs, pre_first, pre_second, labels, classifier, w_first, m_first, v_first, w_second, m_second, v_second):
    kernel = w_second.astype(jnp.bfloat16).reshape(3, 3, CH, CH)
    class_f = classifier.astype(jnp.float32)

    def one_image(carry, item):
        image, first_pre, second_pre, label = item
        hidden = jnp.maximum(first_pre, jnp.zeros_like(first_pre))
        active = jnp.maximum(second_pre, jnp.zeros_like(second_pre))
        logits = jnp.dot(active.reshape(-1, CH), classifier, preferred_element_type=jnp.float32)
        expo = jnp.exp(logits)
        prob = expo / lax.optimization_barrier(jnp.sum(expo, axis=1, keepdims=True))
        onehot = (label.reshape(-1, 1) == jnp.arange(CLASSES, dtype=jnp.int32)[None, :]).astype(jnp.float32)
        dlogit = prob - onehot
        grad_act = jnp.dot(dlogit, class_f.T, precision=lax.Precision.HIGHEST).reshape(second_pre.shape)
        grad_second = jnp.where(second_pre > 0, grad_act, jnp.zeros_like(grad_act)).astype(jnp.bfloat16)
        gw_second = weight_terms(pad_image(hidden), grad_second)
        dhidden = input_terms(pad_image(grad_second), kernel)
        grad_first = jnp.where(first_pre > 0, dhidden, jnp.zeros_like(dhidden)).astype(jnp.bfloat16)
        gw_first = weight_terms(pad_image(image), grad_first)
        return ((carry[0] + gw_first, carry[1] + gw_second), None)
    start = (jnp.zeros((FLAT,), jnp.float32), jnp.zeros((FLAT,), jnp.float32))
    (gw_first, gw_second), unused = lax.scan(one_image, start, (inputs, pre_first, pre_second, labels))
    w1n, m1n, v1n, s1n = lamb_step(gw_first, w_first, m_first, v_first)
    w2n, m2n, v2n, s2n = lamb_step(gw_second, w_second, m_second, v_second)
    return (w1n, m1n, v1n, w2n, m2n, v2n, s1n, s2n)
```

```python
import jax
import jax.numpy as jnp
from jax import lax
from jax.experimental import pallas as pl
from jax.experimental.pallas import tpu as pltpu
from jax.sharding import PartitionSpec as P

STEP = 10

beta_one = 0.9
beta_two = 0.999
epsilon = 1e-06
weight_decay = 0.01
learn_rate = 0.002

MESH = pl.DeviceIdType.MESH
BF = jnp.bfloat16
F32 = jnp.float32
NZ, NA = 8, 4
H, WD, CH = 8, 288, 256
PIX = H * WD
GROUPS = ((1, 3, 5), (0, 0, 3), (2, 5, 8))


def dev(z, x, y, c):
    return {"tile": z, "dp": x * 8 + y * 2 + c}


def rcopy(src, dst, ssem, rsem, where):
    return pltpu.make_async_remote_copy(
        src_ref=src,
        dst_ref=dst,
        send_sem=ssem,
        recv_sem=rsem,
        device_id=where,
        device_id_type=MESH,
    )


def loop(lo, hi, fn):
    lax.fori_loop(lo, hi, lambda i, carry: (fn(i), carry)[1], 0)


def kernel(
    x_hbm, p1_hbm, p2_hbm, lab, c3, w1, m1, v1, w2, m2, v2,
    ow1, om1, ov1, ow2, om2, ov2, os1, os2,
    xv, p1, p2, xt, gs, wsend, g0, ga_, wf, wd,
    st, precv, asend, arecv, bsend, brecv, zsend, zrecv, fsend, frecv, gfin, nbuf, nmid,
    ld, s_g0, r_g0, s_g1, r_g1, s_g2, r_g2, s_g3, r_g3, s_h, r_h,
    s_p, r_p, s_a, r_a, s_b, r_b, s_z, r_z, s_f, r_f, s_n, r_n,
):
    z = lax.axis_index("tile")
    d = lax.axis_index("dp")
    x = d // 8
    y = (d // 2) % 4
    c = d % 2
    a = (1 - c) * x + c * y
    b = (1 - c) * y + c * x

    def ab(aa, bb):
        return dev(z, (1 - c) * aa + c * bb, (1 - c) * bb + c * aa, c)

    cp_p2 = pltpu.make_async_copy(p2_hbm, p2, ld.at[0])
    cp_p1 = pltpu.make_async_copy(p1_hbm, p1, ld.at[1])
    cp_x = pltpu.make_async_copy(x_hbm, xv, ld.at[2])
    cp_p2.start()
    cp_p1.start()
    cp_x.start()

    bar = pltpu.get_barrier_semaphore()

    def sig_zc(i):
        k = (z * 2 + c + i) % 16
        pl.semaphore_signal(bar, inc=1, device_id=dev(k // 2, x, y, k % 2), device_id_type=MESH)

    def sig_xy(i):
        k = (x * 4 + y + i) % 16
        pl.semaphore_signal(bar, inc=1, device_id=dev(z, k // 4, k % 4, c), device_id_type=MESH)

    def sig_tr(i):
        pl.semaphore_signal(bar, inc=1, device_id=dev(i // 2, y, x, i % 2), device_id_type=MESH)

    loop(1, 16, sig_zc)
    loop(1, 16, sig_xy)

    @pl.when(x != y)
    def _():
        loop(0, 16, sig_tr)

    for h in (0, 1):
        wsend[h, 0:9, :] = w2[pl.ds(h, 9, stride=2), :].astype(BF)

    @pl.when(x == y)
    def _():
        pl.semaphore_wait(bar, 30)

    @pl.when(x != y)
    def _():
        pl.semaphore_wait(bar, 46)

    slot = z * 2 + c
    own0 = c == 0
    own1 = jnp.logical_and(c == 1, x == y)

    def g0_copy(h, i):
        where = dev((z + i) % NZ, x, y, 0) if h == 0 else dev((z + i) % NZ, y, x, 1)
        return rcopy(wsend.at[h], g0.at[slot], s_g0.at[h, i], r_g0.at[slot], where)

    for h, own in ((0, own0), (1, own1)):
        loop(1, NZ, lambda i, h=h: g0_copy(h, i).start())

        @pl.when(jnp.logical_not(own))
        def _(h=h):
            g0_copy(h, 0).start()

        @pl.when(own)
        def _(h=h):
            g0[slot] = wsend[h]

    own_any = jnp.logical_or(own0, own1)

    def g0_finish():
        def one(s):
            @pl.when(jnp.logical_not(jnp.logical_and(s == slot, own_any)))
            def _():
                rcopy(g0.at[s], g0.at[s], s_g0.at[0, 0], r_g0.at[s], dev(z, x, y, c)).wait_recv()

        loop(0, 16, one)
        pack = jnp.concatenate([g0[s, 0:16, :].astype(F32)[0:9] for s in range(16)], axis=0)
        ga_[a, b] = pack.astype(BF)

        def send(i):
            rcopy(ga_.at[a, b], ga_.at[a, b], s_g1.at[i], r_g1.at[b], ab(a, (b + i) % NA)).start()

        loop(1, NA, send)

    def g1_finish():
        def wait(i):
            k = (b + i) % NA
            rcopy(ga_.at[a, k], ga_.at[a, k], s_g1.at[i], r_g1.at[k], ab(a, k)).wait_recv()

        loop(1, NA, wait)

        def send(i):
            rcopy(ga_.at[a], ga_.at[a], s_g2.at[i], r_g2.at[a], ab((a + i) % NA, b)).start()

        loop(1, NA, send)

    other = dev(z, x, y, 1 - c)

    def g3_copy():
        return rcopy(wd.at[c], wd.at[c], s_g3, r_g3, other)

    def g2_finish():
        def wait(i):
            k = (a + i) % NA
            rcopy(ga_.at[k], ga_.at[k], s_g2.at[i], r_g2.at[k], ab(k, b)).wait_recv()

        loop(1, NA, wait)

        def unpack(aa):
            base = pl.multiple_of(aa * 72, 8)
            for bb in range(NA):
                block = ga_[aa, bb].astype(F32)
                for zz in range(NZ):
                    wf[pl.ds(base + 288 * zz + 18 * bb, 18), :] = block[18 * zz:18 * zz + 18]

        loop(0, NA, unpack)
        wd[c] = wf[...].astype(BF)
        g3_copy().start()

    cols = lax.broadcasted_iota(jnp.int32, (WD, CH), 0)

    def put_row(layer, row, g):
        at = pl.ds(pl.multiple_of(row * WD, 32), WD)
        gs[layer, 1, at, :] = g.astype(BF)
        gs[layer, 0, at, :] = jnp.where(cols == WD - 1, 0.0, pltpu.roll(g, WD - 1, 0)).astype(BF)
        gs[layer, 2, at, :] = jnp.where(cols == 0, 0.0, pltpu.roll(g, 1, 0)).astype(BF)

    def halo_copy(layer, down):
        src = H if down else 1
        dst = 0 if down else H + 1
        k = 1 if down else 0
        where = dev((z + 1) % NZ, x, y, c) if down else dev((z + NZ - 1) % NZ, x, y, c)
        return rcopy(
            gs.at[layer, 1, pl.ds(src * WD, WD)],
            gs.at[layer, 1, pl.ds(dst * WD, WD)],
            s_h.at[layer, k], r_h.at[layer, k], where,
        )

    def halo_start(layer):
        halo_copy(layer, True).start()
        halo_copy(layer, False).start()

    def halo_finish(layer):
        halo_copy(layer, True).wait_recv()
        halo_copy(layer, False).wait_recv()
        for row, edge in ((0, z == 0), (H + 1, z == NZ - 1)):
            g = gs[layer, 1, pl.ds(row * WD, WD), :].astype(F32)
            put_row(layer, row, jnp.where(edge, 0.0, g))

    cls_row = lax.broadcasted_iota(jnp.int32, (8, WD), 0)
    valid = cls_row < 3

    def second_row(r):
        at = pl.ds(pl.multiple_of(r * WD, 32), WD)
        pre = p2[at, :]
        act = jnp.maximum(pre, jnp.zeros_like(pre))
        logits = lax.dot_general(
            c3[0:16, :], act, (((1,), (1,)), ((), ())), preferred_element_type=F32
        )[0:8]
        top = jnp.max(jnp.where(valid, logits, -1e30), axis=0, keepdims=True)
        expo = jnp.where(valid, jnp.exp(logits - top), 0.0)
        prob = expo / jnp.sum(expo, axis=0, keepdims=True)
        onehot = (cls_row == lab[pl.ds(r, 1), :]).astype(F32)
        dlogit = jnp.where(valid, prob - onehot, 0.0)
        high = dlogit.astype(BF).astype(F32)
        rest = dlogit - high
        mid = rest.astype(BF).astype(F32)
        low = rest - mid
        parts = jnp.concatenate([high, mid, low, jnp.zeros_like(low)], axis=0).astype(BF)
        grad = lax.dot_general(
            parts, c3[...], (((0,), (0,)), ((), ())), preferred_element_type=F32
        )
        put_row(0, r + 1, jnp.where(pre.astype(F32) > 0, grad, 0.0))

    def transpose_in(src, relu):
        def one(k):
            at = pl.ds(pl.multiple_of(k * 256, 256), 256)
            block = src[at, :]
            if relu:
                block = jnp.maximum(block, jnp.zeros_like(block))
            xt[:, at] = block.T

        loop(0, PIX // 256, one)

    def pair_copy(layer, group):
        dy = GROUPS[group][0]
        rows = pl.ds(dy * 768, 768)
        return rcopy(
            st.at[layer, 1 - c, rows], precv.at[layer, rows],
            s_p.at[layer, group], r_p.at[layer, group], other,
        )

    def taps(layer, group):
        dy = GROUPS[group][0]

        def one(dx):
            window = gs[layer, dx, pl.ds((2 - dy) * WD, PIX), :]
            part = lax.dot_general(
                xt[...], window, (((1,), (0,)), ((), ())), preferred_element_type=F32
            )
            at = pl.ds(pl.multiple_of((dy * 3 + dx) * 256, 256), 256)
            st[layer, 0, at, :] = part[:, 0:128]
            st[layer, 1, at, :] = part[:, 128:256]

        loop(0, 3, one)
        pair_copy(layer, group).start()

    def a_copy(layer, group, i):
        _, z0, z1 = GROUPS[group]
        k = (a + i) % NA
        return rcopy(
            asend.at[layer, k, pl.ds(z0, z1 - z0)], arecv.at[layer, a, pl.ds(z0, z1 - z0)],
            s_a.at[layer, group, i], r_a.at[layer, group, a], ab(k, b),
        )

    def a_start(layer, group):
        pair_copy(layer, group).wait_recv()
        _, z0, z1 = GROUPS[group]

        def one(zz):
            for aa in range(NA):
                at = pl.ds(pl.multiple_of(zz * 288 + aa * 72, 8), 72)
                asend[layer, aa, zz, 0:72, :] = (st[layer, c, at, :] + precv[layer, at, :]).astype(BF)

        loop(z0, z1, one)
        loop(1, NA, lambda i: a_copy(layer, group, i).start())

    def b_copy(layer, i):
        k = (b + i) % NA
        return rcopy(
            bsend.at[layer, k], brecv.at[layer, b],
            s_b.at[layer, i], r_b.at[layer, b], ab(a, k),
        )

    def a_finish(layer):
        for group in range(3):
            _, z0, z1 = GROUPS[group]

            def wait(i, group=group, z0=z0, z1=z1):
                k = (a + i) % NA
                ref = arecv.at[layer, k, pl.ds(z0, z1 - z0)]
                rcopy(ref, ref, s_a.at[layer, group, i], r_a.at[layer, group, k], ab(k, b)).wait_recv()

            loop(1, NA, wait)

        def one(zz):
            at = pl.ds(pl.multiple_of(zz * 288 + a * 72, 8), 72)
            total = st[layer, c, at, :] + precv[layer, at, :]
            for i in range(1, NA):
                total = total + arecv[layer, (a + i) % NA, zz, 0:72, :].astype(F32)
            for bb in range(NA):
                bsend[layer, bb, zz, 0:18, :] = total[18 * bb:18 * bb + 18]

        loop(0, NZ, one)
        loop(1, NA, lambda i: b_copy(layer, i).start())

    def z_copy(layer, i):
        k = (z + i) % NZ
        return rcopy(
            zsend.at[layer, k], zrecv.at[layer, z],
            s_z.at[layer, i], r_z.at[layer, z], dev(k, x, y, c),
        )

    def b_finish(layer):
        def wait(i):
            k = (b + i) % NA
            rcopy(
                brecv.at[layer, k], brecv.at[layer, k], s_b.at[layer, i], r_b.at[layer, k], ab(a, k)
            ).wait_recv()

        loop(1, NA, wait)

        def one(zz):
            total = bsend[layer, b, zz, 0:18, :]
            for i in range(1, NA):
                total = total + brecv[layer, (b + i) % NA, zz, 0:18, :]
            zsend[layer, zz, 0:18, :] = total

        loop(0, NZ, one)
        loop(1, NZ, lambda i: z_copy(layer, i).start())

    def f_own(cc):
        return own0 if cc == 0 else own1

    def f_copy(layer, cc):
        return rcopy(
            fsend.at[layer, cc], frecv.at[layer, c],
            s_f.at[layer, cc], r_f.at[layer, c], dev(z, a, b, cc),
        )

    def z_finish(layer):
        def wait(i):
            k = (z + i) % NZ
            rcopy(
                zrecv.at[layer, k], zrecv.at[layer, k],
                s_z.at[layer, i], r_z.at[layer, k], dev(k, x, y, c),
            ).wait_recv()

        loop(1, NZ, wait)
        total = zsend[layer, z, 0:18, :]
        for i in range(1, NZ):
            total = total + zrecv[layer, (z + i) % NZ, 0:18, :]
        for cc in range(2):
            fsend[layer, cc, 0:9, :] = total[9 * cc:9 * cc + 9]

            @pl.when(jnp.logical_not(f_own(cc)))
            def _(cc=cc):
                f_copy(layer, cc).start()

            @pl.when(f_own(cc))
            def _(cc=cc):
                frecv[layer, c] = fsend[layer, cc]

    def f_finish(layer):
        for cc in range(2):
            @pl.when(jnp.logical_not(f_own(cc)))
            def _(cc=cc):
                ref = frecv.at[layer, cc]
                rcopy(ref, ref, s_f.at[layer, cc], r_f.at[layer, cc], dev(z, a, b, cc)).wait_recv()

            gfin[layer, pl.ds(cc, 9, stride=2), :] = frecv[layer, cc, 0:9, :]
        return gfin[layer]

    def moments(grad, weight, first, second):
        first_new = beta_one * first + (1.0 - beta_one) * grad
        second_new = beta_two * second + (1.0 - beta_two) * grad * grad
        corr_one = 1.0 - beta_one**STEP
        corr_two = 1.0 - beta_two**STEP
        update = (
            first_new / corr_one / (jnp.sqrt(second_new / corr_two) + epsilon)
            + weight_decay * weight
        )
        return (first_new, second_new, update)

    def first_row(r):
        total = jnp.zeros((WD, CH), F32)
        for dy in range(3):
            at = pl.ds(pl.multiple_of((r + 2 - dy) * WD, 32), WD)
            for dx in range(3):
                t = (dy * 3 + dx) * 256
                tap = jnp.concatenate([wd[0, t:t + 256, :], wd[1, t:t + 256, :]], axis=1)
                total = total + lax.dot_general(
                    gs[0, dx, at, :], tap, (((1,), (1,)), ((), ())), preferred_element_type=F32
                )
        pre = p1[pl.ds(pl.multiple_of(r * WD, 32), WD), :]
        put_row(1, r + 1, jnp.where(pre.astype(F32) > 0, total, 0.0))

    cp_p2.wait()
    loop(0, 2, lambda i: second_row(i * (H - 1)))
    halo_start(0)
    g0_finish()
    loop(1, H - 1, second_row)
    g1_finish()
    cp_p1.wait()
    transpose_in(p1, True)
    taps(0, 0)
    g2_finish()
    halo_finish(0)
    taps(0, 1)
    a_start(0, 0)
    taps(0, 2)
    a_start(0, 1)
    cp_x.wait()
    transpose_in(xv, False)
    a_start(0, 2)
    g3_copy().wait_recv()
    loop(0, 2, lambda i: first_row(i * (H - 1)))
    halo_start(1)
    loop(1, H - 1, first_row)
    a_finish(0)
    taps(1, 0)
    b_finish(0)
    halo_finish(1)
    taps(1, 1)
    a_start(1, 0)
    z_finish(0)
    taps(1, 2)
    a_start(1, 1)
    m2n, v2n, u2 = moments(f_finish(0), w2[...], m2[...], v2[...])
    om2[...] = m2n
    ov2[...] = v2n
    os2[...] = u2
    a_start(1, 2)
    a_finish(1)
    b_finish(1)
    z_finish(1)
    m1n, v1n, u1 = moments(f_finish(1), w1[...], m1[...], v1[...])
    om1[...] = m1n
    ov1[...] = v1n

    def squares(value):
        return jnp.sum(value * value, axis=0, keepdims=True)

    u2 = os2[...]
    nbuf[0, slot] = jnp.concatenate(
        [squares(w1[...]), squares(u1), squares(w2[...]), squares(u2), jnp.zeros((4, 128), F32)],
        axis=0,
    )
    place = x * 4 + y

    def n_copy(stage, i):
        if stage == 0:
            k = (slot + i) % 16
            return rcopy(
                nbuf.at[0, slot], nbuf.at[0, slot], s_n.at[0, i], r_n.at[0, slot],
                dev(k // 2, x, y, k % 2),
            )
        k = (place + i) % 16
        return rcopy(
            nbuf.at[1, place], nbuf.at[1, place], s_n.at[1, i], r_n.at[1, place],
            dev(z, k // 4, k % 4, c),
        )

    def n_wait(stage, i):
        k = ((slot if stage == 0 else place) + i) % 16
        ref = nbuf.at[stage, k]
        rcopy(ref, ref, s_n.at[stage, i], r_n.at[stage, k], other).wait_recv()

    loop(1, 16, lambda i: n_copy(0, i).start())
    loop(1, 16, lambda i: n_wait(0, i))
    nbuf[1, place] = jnp.sum(nbuf[0], axis=0)
    loop(1, 16, lambda i: n_copy(1, i).start())
    loop(1, 16, lambda i: n_wait(1, i))
    sums = jnp.sqrt(jnp.sum(jnp.sum(nbuf[1], axis=0), axis=1, keepdims=True))
    step1 = sums[0:1] / sums[1:2] * u1
    step2 = sums[2:3] / sums[3:4] * u2
    os1[...] = step1
    os2[...] = step2
    ow1[...] = w1[...] - learn_rate * step1
    ow2[...] = w2[...] - learn_rate * step2

    for h, own in ((0, own0), (1, own1)):
        loop(1, NZ, lambda i, h=h: g0_copy(h, i).wait_send())

        @pl.when(jnp.logical_not(own))
        def _(h=h):
            g0_copy(h, 0).wait_send()

    def done(i):
        rcopy(ga_.at[a, b], ga_.at[a, b], s_g1.at[i], r_g1.at[b], other).wait_send()
        rcopy(ga_.at[a], ga_.at[a], s_g2.at[i], r_g2.at[a], other).wait_send()
        for layer in range(2):
            for group in range(3):
                a_copy(layer, group, i).wait_send()
            b_copy(layer, i).wait_send()

    loop(1, NA, done)
    g3_copy().wait_send()
    for layer in range(2):
        halo_copy(layer, True).wait_send()
        halo_copy(layer, False).wait_send()
        for group in range(3):
            pair_copy(layer, group).wait_send()
        loop(1, NZ, lambda i, layer=layer: z_copy(layer, i).wait_send())
        for cc in range(2):
            @pl.when(jnp.logical_not(f_own(cc)))
            def _(cc=cc, layer=layer):
                f_copy(layer, cc).wait_send()

    for stage in range(2):
        loop(1, 16, lambda i, stage=stage: n_copy(stage, i).wait_send())


def body(
    inputs, pre_first, pre_second, labels, classifier,
    w_first, m_first, v_first, w_second, m_second, v_second,
):
    flat = [t.reshape(18, 128) for t in (w_first, m_first, v_first, w_second, m_second, v_second)]
    c3 = jnp.tile(jnp.pad(classifier.T, ((0, 5), (0, 0))), (4, 1))
    vm = pl.BlockSpec(memory_space=pltpu.VMEM)
    hb = pl.BlockSpec(memory_space=pl.ANY)
    dma = pltpu.SemaphoreType.DMA
    outs = pl.pallas_call(
        kernel,
        out_shape=[jax.ShapeDtypeStruct((18, 128), F32)] * 8,
        in_specs=[hb] * 3 + [vm] * 8,
        out_specs=[vm] * 8,
        scratch_shapes=[
            pltpu.VMEM((PIX, CH), BF),
            pltpu.VMEM((PIX, CH), BF),
            pltpu.VMEM((PIX, CH), BF),
            pltpu.VMEM((CH, PIX), BF),
            pltpu.VMEM((2, 3, (H + 2) * WD, CH), BF),
            pltpu.VMEM((2, 16, 128), BF),
            pltpu.VMEM((16, 16, 128), BF),
            pltpu.VMEM((NA, NA, 144, 128), BF),
            pltpu.VMEM((2304, 128), F32),
            pltpu.VMEM((2, 2304, 128), BF),
            pltpu.VMEM((2, 2, 2304, 128), F32),
            pltpu.VMEM((2, 2304, 128), F32),
            pltpu.VMEM((2, NA, NZ, 80, 128), BF),
            pltpu.VMEM((2, NA, NZ, 80, 128), BF),
            pltpu.VMEM((2, NA, NZ, 24, 128), F32),
            pltpu.VMEM((2, NA, NZ, 24, 128), F32),
            pltpu.VMEM((2, NZ, 24, 128), F32),
            pltpu.VMEM((2, NZ, 24, 128), F32),
            pltpu.VMEM((2, 2, 16, 128), F32),
            pltpu.VMEM((2, 2, 16, 128), F32),
            pltpu.VMEM((2, 18, 128), F32),
            pltpu.VMEM((2, 16, 8, 128), F32),
            pltpu.VMEM((8, 128), F32),
            dma((3,)),
            dma((2, NZ)), dma((16,)),
            dma((NA,)), dma((NA,)),
            dma((NA,)), dma((NA,)),
            dma, dma,
            dma((2, 2)), dma((2, 2)),
            dma((2, 3)), dma((2, 3)),
            dma((2, 3, NA)), dma((2, 3, NA)),
            dma((2, NA)), dma((2, NA)),
            dma((2, NZ)), dma((2, NZ)),
            dma((2, 2)), dma((2, 2)),
            dma((2, 16)), dma((2, 16)),
        ],
        compiler_params=pltpu.CompilerParams(
            collective_id=0, has_side_effects=True, vmem_limit_bytes=56 * 1024 * 1024
        ),
        cost_estimate=pl.CostEstimate(
            flops=2 * 27 * PIX * CH * CH, bytes_accessed=4_000_000, transcendentals=3 * PIX
        ),
    )(
        inputs.reshape(PIX, CH), pre_first.reshape(PIX, CH), pre_second.reshape(PIX, CH),
        labels[0], c3, *flat,
    )
    return tuple(t.reshape(2304) for t in outs)


def solution(mesh):
    grid = P("dp", "tile", None, None)
    flat = P(("tile", "dp"))
    return jax.shard_map(
        body,
        mesh=mesh,
        in_specs=(grid, grid, grid, P("dp", "tile", None), P(), flat, flat, flat, flat, flat, flat),
        out_specs=(flat,) * 8,
        check_vma=False,
    )
```

```python
import jax
import jax.numpy as jnp
from jax import lax
from jax.experimental import pallas as pl
from jax.experimental.pallas import tpu as pltpu
from jax.sharding import PartitionSpec as P

STEP = 10

beta_one = 0.9
beta_two = 0.999
epsilon = 1e-06
weight_decay = 0.01
learn_rate = 0.002

MESH = pl.DeviceIdType.MESH
BF = jnp.bfloat16
F32 = jnp.float32
NZ, NA = 8, 4
H, WD, CH = 8, 288, 256
PIX = H * WD
GROUPS = (1, 0, 2)
PARTS = (((0, 1), (3, 4, 0, 1, 2), 0, 1440), ((2,), (5, 6, 7), 1440, 2304))


def dev(z, x, y, c):
    return {"tile": z, "dp": x * 8 + y * 2 + c}


def rcopy(src, dst, ssem, rsem, where):
    return pltpu.make_async_remote_copy(
        src_ref=src,
        dst_ref=dst,
        send_sem=ssem,
        recv_sem=rsem,
        device_id=where,
        device_id_type=MESH,
    )


def loop(lo, hi, fn):
    lax.fori_loop(lo, hi, lambda i, carry: (fn(i), carry)[1], 0)


def kernel(
    x_hbm, p1_hbm, p2_hbm, lab, ct, w1, m1, v1, w2, m2, v2,
    outs,
    xv, p1, p2, xt, gs, c3, wsend, g0, ga_, wf, wd,
    st, precv, tot, asend0, arecv0, asend1, arecv1, zsend, zrecv, gfin, nbuf,
    ld, s_g0, r_g0, s_g1, r_g1, s_g2, r_g2, s_g3, r_g3, s_h, r_h,
    s_p, r_p, s_a, r_a, s_z, r_z, s_n, r_n,
):
    z = lax.axis_index("tile")
    d = lax.axis_index("dp")
    x = d // 8
    y = (d // 2) % 4
    c = d % 2
    a = (1 - c) * x + c * y
    b = (1 - c) * y + c * x

    def ab(aa, bb):
        return dev(z, (1 - c) * aa + c * bb, (1 - c) * bb + c * aa, c)

    cp_p2 = pltpu.make_async_copy(p2_hbm, p2, ld.at[0])
    cp_p1 = pltpu.make_async_copy(p1_hbm, p1, ld.at[1])
    cp_x = pltpu.make_async_copy(x_hbm, xv, ld.at[2])
    cp_p2.start()
    cp_p1.start()
    cp_x.start()

    bar = pltpu.get_barrier_semaphore()

    def sig_zc(i):
        k = (z * 2 + c + i) % 16
        pl.semaphore_signal(bar, inc=1, device_id=dev(k // 2, x, y, k % 2), device_id_type=MESH)

    def sig_xy(i):
        k = (x * 4 + y + i) % 16
        pl.semaphore_signal(bar, inc=1, device_id=dev(z, k // 4, k % 4, c), device_id_type=MESH)

    loop(1, 16, sig_zc)
    loop(1, 16, sig_xy)

    for h in (0, 1):
        wsend[h, 0:9, :] = w2[pl.ds(h, 9, stride=2), :].astype(BF)

    table = jnp.concatenate([ct[...].astype(F32), jnp.zeros((5, CH), F32)], axis=0)
    c3[...] = jnp.concatenate([table] * 4, axis=0).astype(BF)

    slot = z * 2 + c
    place = x * 4 + y

    def g0_copy(i):
        k = (slot + i) % 16
        return rcopy(
            wsend.at[k % 2], g0.at[slot], s_g0.at[i], r_g0.at[slot], dev(k // 2, x, y, k % 2)
        )

    def g0_start():
        g0[slot] = wsend[c]
        loop(1, 16, lambda i: g0_copy(i).start())

    def g1_copy(i):
        return rcopy(
            ga_.at[a, b], ga_.at[a, b], s_g1.at[i], r_g1.at[b], ab(a, (b + i) % NA)
        )

    def g2_copy(k, i):
        return rcopy(
            ga_.at[a, k], ga_.at[a, k], s_g2.at[k, i], r_g2.at[a, k], ab((a + i) % NA, b)
        )

    def g0_finish():
        def one(i):
            k = (slot + i) % 16
            rcopy(g0.at[k], g0.at[k], s_g0.at[i], r_g0.at[k], dev(z, x, y, c)).wait_recv()

        loop(1, 16, one)
        pack = jnp.concatenate([g0[s, 0:16, :].astype(F32)[0:9] for s in range(16)], axis=0)
        ga_[a, b] = pack.astype(BF)
        loop(1, NA, lambda i: g1_copy(i).start())
        loop(1, NA, lambda i: g2_copy(b, i).start())

    def g1_finish():
        for j in (1, 3, 2):
            k = (b + j) % NA
            rcopy(ga_.at[a, k], ga_.at[a, k], s_g1.at[j], r_g1.at[k], ab(a, k)).wait_recv()
            loop(1, NA, lambda i, k=k: g2_copy(k, i).start())

    other = dev(z, x, y, 1 - c)

    def g3_copy():
        return rcopy(wd.at[c], wd.at[c], s_g3, r_g3, other)

    def g2_finish():
        def wait(i):
            k = (a + i) % NA
            for j in range(NA):
                rcopy(
                    ga_.at[k, j], ga_.at[k, j], s_g2.at[j, i], r_g2.at[k, j], ab(k, b)
                ).wait_recv()

        loop(1, NA, wait)

        def unpack(xx):
            base = pl.multiple_of(xx * 72, 8)
            for yy in range(NA):
                block = ga_[(1 - c) * xx + c * yy, (1 - c) * yy + c * xx].astype(F32)
                for zz in range(NZ):
                    wf[pl.ds(base + 288 * zz + 18 * yy, 18), :] = block[18 * zz:18 * zz + 18]

        loop(0, NA, unpack)
        wd[c] = wf[...].astype(BF)
        g3_copy().start()

    cols = lax.broadcasted_iota(jnp.int32, (WD, CH), 0)

    def put_row(layer, row, g):
        at = pl.ds(pl.multiple_of(row * WD, 32), WD)
        gs[layer, 1, at, :] = g.astype(BF)
        gs[layer, 0, at, :] = jnp.where(cols == WD - 1, 0.0, pltpu.roll(g, WD - 1, 0)).astype(BF)
        gs[layer, 2, at, :] = jnp.where(cols == 0, 0.0, pltpu.roll(g, 1, 0)).astype(BF)

    def halo_copy(layer, down):
        src = H if down else 1
        dst = 0 if down else H + 1
        k = 1 if down else 0
        where = dev((z + 1) % NZ, x, y, c) if down else dev((z + NZ - 1) % NZ, x, y, c)
        return rcopy(
            gs.at[layer, 1, pl.ds(src * WD, WD)],
            gs.at[layer, 1, pl.ds(dst * WD, WD)],
            s_h.at[layer, k], r_h.at[layer, k], where,
        )

    def halo_start(layer):
        halo_copy(layer, True).start()
        halo_copy(layer, False).start()

    def halo_finish(layer):
        halo_copy(layer, True).wait_recv()
        halo_copy(layer, False).wait_recv()
        for row, edge in ((0, z == 0), (H + 1, z == NZ - 1)):
            g = gs[layer, 1, pl.ds(row * WD, WD), :].astype(F32)
            put_row(layer, row, jnp.where(edge, 0.0, g))

    cls_row = lax.broadcasted_iota(jnp.int32, (8, WD), 0)
    valid = cls_row < 3

    def second_row(r):
        at = pl.ds(pl.multiple_of(r * WD, 32), WD)
        pre = p2[at, :]
        act = jnp.maximum(pre, jnp.zeros_like(pre))
        logits = lax.dot_general(
            c3[0:16, :], act, (((1,), (1,)), ((), ())), preferred_element_type=F32
        )[0:8]
        top = jnp.max(jnp.where(valid, logits, -1e30), axis=0, keepdims=True)
        expo = jnp.where(valid, jnp.exp(logits - top), 0.0)
        prob = expo / jnp.sum(expo, axis=0, keepdims=True)
        onehot = (cls_row == lab[pl.ds(r, 1), :]).astype(F32)
        dlogit = jnp.where(valid, prob - onehot, 0.0)
        high = dlogit.astype(BF).astype(F32)
        rest = dlogit - high
        mid = rest.astype(BF).astype(F32)
        low = rest - mid
        parts = jnp.concatenate([high, mid, low, jnp.zeros_like(low)], axis=0).astype(BF)
        grad = lax.dot_general(
            parts, c3[...], (((0,), (0,)), ((), ())), preferred_element_type=F32
        )
        put_row(0, r + 1, jnp.where(pre.astype(F32) > 0, grad, 0.0))

    def transpose_in(src, relu):
        def one(k):
            at = pl.ds(pl.multiple_of(k * 256, 256), 256)
            block = src[at, :]
            if relu:
                block = jnp.maximum(block, jnp.zeros_like(block))
            xt[:, at] = block.T

        loop(0, PIX // 256, one)

    def pair_copy(layer, group):
        dy = GROUPS[group]
        rows = pl.ds(dy * 768, 768)
        return rcopy(
            st.at[layer, 1 - c, rows], precv.at[layer, rows],
            s_p.at[layer, group], r_p.at[layer, group], other,
        )

    def taps(layer, group):
        dy = GROUPS[group]

        def one(dx):
            window = gs[layer, dx, pl.ds((2 - dy) * WD, PIX), :]
            part = lax.dot_general(
                xt[...], window, (((1,), (0,)), ((), ())), preferred_element_type=F32
            )
            at = pl.ds(pl.multiple_of((dy * 3 + dx) * 256, 256), 256)
            st[layer, 0, at, :] = part[:, 0:128]
            st[layer, 1, at, :] = part[:, 128:256]

        loop(0, 3, one)
        pair_copy(layer, group).start()

    def pack_refs(part):
        return (asend0, arecv0) if part == 0 else (asend1, arecv1)

    def a_copy(layer, part, i):
        send, recv = pack_refs(part)
        k = (place + i) % 16
        return rcopy(
            send.at[layer, k], recv.at[layer, place],
            s_a.at[layer, part, i], r_a.at[layer, part, place], dev(z, k // 4, k % 4, c),
        )

    def a_start(layer, part):
        for group in PARTS[part][0]:
            pair_copy(layer, group).wait_recv()
        _, zs, lo, hi = PARTS[part]
        tot[lo:hi, :] = st[layer, c, lo:hi, :] + precv[layer, lo:hi, :]
        send = pack_refs(part)[0]
        rows = 18 * len(zs)

        def one(xx):
            base = pl.multiple_of(xx * 72, 8)
            for yy in range(NA):
                block = jnp.concatenate(
                    [tot[pl.ds(base + 288 * zz + 18 * yy, 18), :] for zz in zs]
                    + [jnp.zeros((send.shape[2] - rows, 128), F32)],
                    axis=0,
                )
                send[layer, xx * 4 + yy] = block.astype(BF)

        loop(0, NA, one)
        loop(1, 16, lambda i: a_copy(layer, part, i).start())

    def z_copy(layer, i):
        k = (slot + i) % 16
        return rcopy(
            zsend.at[layer, k], zrecv.at[layer, slot],
            s_z.at[layer, i], r_z.at[layer, slot], dev(k // 2, x, y, k % 2),
        )

    def a_finish(layer):
        for part in range(2):
            send, recv = pack_refs(part)

            def wait(i, part=part, recv=recv):
                k = (place + i) % 16
                rcopy(
                    recv.at[layer, k], recv.at[layer, k],
                    s_a.at[layer, part, i], r_a.at[layer, part, k], other,
                ).wait_recv()

            loop(1, 16, wait)
            total = lax.fori_loop(
                1, 16,
                lambda i, acc, recv=recv: acc + recv[layer, (place + i) % 16].astype(F32),
                send[layer, place].astype(F32),
            )
            for j, zz in enumerate(PARTS[part][1]):
                for cc in range(2):
                    r = 18 * j + 9 * cc
                    zsend[layer, 2 * zz + cc, 0:9, :] = total[r:r + 9]

        zrecv[layer, slot] = zsend[layer, slot]
        loop(1, 16, lambda i: z_copy(layer, i).start())

    def z_finish(layer):
        def wait(i):
            k = (slot + i) % 16
            rcopy(
                zrecv.at[layer, k], zrecv.at[layer, k],
                s_z.at[layer, i], r_z.at[layer, k], other,
            ).wait_recv()

        loop(1, 16, wait)
        for cc in range(2):
            total = zrecv[layer, cc, 0:9, :]
            for zz in range(1, NZ):
                total = total + zrecv[layer, 2 * zz + cc, 0:9, :]
            gfin[layer, pl.ds(cc, 9, stride=2), :] = total
        return gfin[layer]

    def moments(grad, weight, first, second):
        first_new = beta_one * first + (1.0 - beta_one) * grad
        second_new = beta_two * second + (1.0 - beta_two) * grad * grad
        corr_one = 1.0 - beta_one**STEP
        corr_two = 1.0 - beta_two**STEP
        update = (
            first_new / corr_one / (jnp.sqrt(second_new / corr_two) + epsilon)
            + weight_decay * weight
        )
        return (first_new, second_new, update)

    def first_row(r):
        total = jnp.zeros((WD, CH), F32)
        for dy in range(3):
            at = pl.ds(pl.multiple_of((r + 2 - dy) * WD, 32), WD)
            for dx in range(3):
                t = (dy * 3 + dx) * 256
                tap = jnp.concatenate([wd[0, t:t + 256, :], wd[1, t:t + 256, :]], axis=1)
                total = total + lax.dot_general(
                    gs[0, dx, at, :], tap, (((1,), (1,)), ((), ())), preferred_element_type=F32
                )
        pre = p1[pl.ds(pl.multiple_of(r * WD, 32), WD), :]
        put_row(1, r + 1, jnp.where(pre.astype(F32) > 0, total, 0.0))

    cp_p2.wait()
    loop(0, 2, lambda i: second_row(i * (H - 1)))
    pl.semaphore_wait(bar, 30)
    g0_start()
    halo_start(0)
    loop(1, H - 1, second_row)
    g0_finish()
    cp_p1.wait()
    transpose_in(p1, True)
    taps(0, 0)
    g1_finish()
    halo_finish(0)
    taps(0, 1)
    taps(0, 2)
    cp_x.wait()
    transpose_in(xv, False)
    g2_finish()
    a_start(0, 0)
    a_start(0, 1)
    g3_copy().wait_recv()
    loop(0, 2, lambda i: first_row(i * (H - 1)))
    halo_start(1)
    loop(1, H - 1, first_row)
    taps(1, 0)
    halo_finish(1)
    taps(1, 1)
    a_start(1, 0)
    taps(1, 2)
    a_start(1, 1)
    a_finish(0)
    a_finish(1)
    m2n, v2n, u2 = moments(z_finish(0), w2[...], m2[...], v2[...])
    outs[4, 0:18, :] = m2n
    outs[5, 0:18, :] = v2n
    outs[7, 0:18, :] = u2
    m1n, v1n, u1 = moments(z_finish(1), w1[...], m1[...], v1[...])
    outs[1, 0:18, :] = m1n
    outs[2, 0:18, :] = v1n

    def squares(value):
        return jnp.sum(value * value, axis=0, keepdims=True)

    u2 = outs[7, 0:18, :]
    nbuf[0, slot] = jnp.concatenate(
        [squares(w1[...]), squares(u1), squares(w2[...]), squares(u2), jnp.zeros((4, 128), F32)],
        axis=0,
    )
    def n_copy(stage, i):
        if stage == 0:
            k = (slot + i) % 16
            return rcopy(
                nbuf.at[0, slot], nbuf.at[0, slot], s_n.at[0, i], r_n.at[0, slot],
                dev(k // 2, x, y, k % 2),
            )
        k = (place + i) % 16
        return rcopy(
            nbuf.at[1, place], nbuf.at[1, place], s_n.at[1, i], r_n.at[1, place],
            dev(z, k // 4, k % 4, c),
        )

    def n_wait(stage, i):
        k = ((slot if stage == 0 else place) + i) % 16
        ref = nbuf.at[stage, k]
        rcopy(ref, ref, s_n.at[stage, i], r_n.at[stage, k], other).wait_recv()

    loop(1, 16, lambda i: n_copy(0, i).start())
    loop(1, 16, lambda i: n_wait(0, i))
    nbuf[1, place] = jnp.sum(nbuf[0], axis=0)
    loop(1, 16, lambda i: n_copy(1, i).start())
    loop(1, 16, lambda i: n_wait(1, i))
    sums = jnp.sqrt(jnp.sum(jnp.sum(nbuf[1], axis=0), axis=1, keepdims=True))
    step1 = sums[0:1] / sums[1:2] * u1
    step2 = sums[2:3] / sums[3:4] * u2
    outs[6, 0:18, :] = step1
    outs[7, 0:18, :] = step2
    outs[0, 0:18, :] = w1[...] - learn_rate * step1
    outs[3, 0:18, :] = w2[...] - learn_rate * step2

    def done(i):
        g0_copy(i).wait_send()
        for layer in range(2):
            for part in range(2):
                a_copy(layer, part, i).wait_send()
            z_copy(layer, i).wait_send()
        for stage in range(2):
            n_copy(stage, i).wait_send()

    loop(1, 16, done)

    def done_gather(i):
        g1_copy(i).wait_send()
        for k in range(NA):
            g2_copy(k, i).wait_send()

    loop(1, NA, done_gather)
    g3_copy().wait_send()
    for layer in range(2):
        halo_copy(layer, True).wait_send()
        halo_copy(layer, False).wait_send()
        for group in range(3):
            pair_copy(layer, group).wait_send()


def body(
    inputs, pre_first, pre_second, labels, classifier,
    w_first, m_first, v_first, w_second, m_second, v_second,
):
    flat = [t.reshape(18, 128) for t in (w_first, m_first, v_first, w_second, m_second, v_second)]
    vm = pl.BlockSpec(memory_space=pltpu.VMEM)
    hb = pl.BlockSpec(memory_space=pl.ANY)
    dma = pltpu.SemaphoreType.DMA
    outs = pl.pallas_call(
        kernel,
        out_shape=jax.ShapeDtypeStruct((8, 24, 128), F32),
        in_specs=[hb] * 3 + [vm] * 8,
        out_specs=vm,
        scratch_shapes=[
            pltpu.VMEM((PIX, CH), BF),
            pltpu.VMEM((PIX, CH), BF),
            pltpu.VMEM((PIX, CH), BF),
            pltpu.VMEM((CH, PIX), BF),
            pltpu.VMEM((2, 3, (H + 2) * WD, CH), BF),
            pltpu.VMEM((32, CH), BF),
            pltpu.VMEM((2, 16, 128), BF),
            pltpu.VMEM((16, 16, 128), BF),
            pltpu.VMEM((NA, NA, 144, 128), BF),
            pltpu.VMEM((2304, 128), F32),
            pltpu.VMEM((2, 2304, 128), BF),
            pltpu.VMEM((2, 2, 2304, 128), F32),
            pltpu.VMEM((2, 2304, 128), F32),
            pltpu.VMEM((2304, 128), F32),
            pltpu.VMEM((2, 16, 96, 128), BF),
            pltpu.VMEM((2, 16, 96, 128), BF),
            pltpu.VMEM((2, 16, 64, 128), BF),
            pltpu.VMEM((2, 16, 64, 128), BF),
            pltpu.VMEM((2, 16, 16, 128), F32),
            pltpu.VMEM((2, 16, 16, 128), F32),
            pltpu.VMEM((2, 18, 128), F32),
            pltpu.VMEM((2, 16, 8, 128), F32),
            dma((3,)),
            dma((16,)), dma((16,)),
            dma((NA,)), dma((NA,)),
            dma((NA, NA)), dma((NA, NA)),
            dma, dma,
            dma((2, 2)), dma((2, 2)),
            dma((2, 3)), dma((2, 3)),
            dma((2, 2, 16)), dma((2, 2, 16)),
            dma((2, 16)), dma((2, 16)),
            dma((2, 16)), dma((2, 16)),
        ],
        compiler_params=pltpu.CompilerParams(
            collective_id=0, has_side_effects=True, vmem_limit_bytes=56 * 1024 * 1024
        ),
        cost_estimate=pl.CostEstimate(
            flops=2 * 27 * PIX * CH * CH, bytes_accessed=4_000_000, transcendentals=3 * PIX
        ),
    )(
        inputs.reshape(PIX, CH), pre_first.reshape(PIX, CH), pre_second.reshape(PIX, CH),
        labels[0], classifier.T, *flat,
    )
    return tuple(outs[i, 0:18].reshape(2304) for i in range(8))


def solution(mesh):
    grid = P("dp", "tile", None, None)
    flat = P(("tile", "dp"))
    return jax.shard_map(
        body,
        mesh=mesh,
        in_specs=(grid, grid, grid, P("dp", "tile", None), P(), flat, flat, flat, flat, flat, flat),
        out_specs=(flat,) * 8,
        check_vma=False,
    )
```

```python
import jax
import jax.numpy as jnp
from jax import lax
from jax.experimental import pallas as pl
from jax.experimental.pallas import tpu as pltpu
from jax.sharding import PartitionSpec as P

STEP = 10

beta_one = 0.9
beta_two = 0.999
epsilon = 1e-06
weight_decay = 0.01
learn_rate = 0.002

MESH = pl.DeviceIdType.MESH
BF = jnp.bfloat16
F32 = jnp.float32
NZ, NA = 8, 4
H, WD, CH = 8, 288, 256
PIX = H * WD
GROUPS = (1, 0, 2)
ZORDER = (3, 4, 0, 1, 2, 5, 6, 7)
PARTS = ((0, 32, 0, (768, 1536)), (32, 80, 1, (0, 768)), (80, 144, 2, (1536, 2304)))


def pieces(lo, hi):
    cut = []
    for j, zz in enumerate(ZORDER):
        first, last = max(lo, 18 * j), min(hi, 18 * j + 18)
        if first < last:
            cut.append((zz, first - 18 * j, last - first))
    return cut


def dev(z, x, y, c):
    return {"tile": z, "dp": x * 8 + y * 2 + c}


def rcopy(src, dst, ssem, rsem, where):
    return pltpu.make_async_remote_copy(
        src_ref=src,
        dst_ref=dst,
        send_sem=ssem,
        recv_sem=rsem,
        device_id=where,
        device_id_type=MESH,
    )


def loop(lo, hi, fn):
    lax.fori_loop(lo, hi, lambda i, carry: (fn(i), carry)[1], 0)


def kernel(
    x_hbm, p1_hbm, p2_hbm, lab_hbm, ct_hbm, w1_hbm, m1_hbm, v1_hbm, w2_hbm, m2_hbm, v2_hbm,
    outs,
    lab, ct, w1, m1, v1, w2, m2, v2, xv, p1, p2, xt, gs, c3, wsend, g0, ga_, wf, wd,
    st, precv, tot, asend, arecv, asum, zsend, zrecv, gfin, nbuf,
    ld, s_g0, r_g0, s_g1, r_g1, s_g2, r_g2, s_g3, r_g3, s_h, r_h,
    s_p, r_p, s_a, r_a, s_z, r_z, s_n, r_n,
):
    z = lax.axis_index("tile")
    d = lax.axis_index("dp")
    x = d // 8
    y = (d // 2) % 4
    c = d % 2
    a = (1 - c) * x + c * y
    b = (1 - c) * y + c * x

    def ab(aa, bb):
        return dev(z, (1 - c) * aa + c * bb, (1 - c) * bb + c * aa, c)

    cp_p2 = pltpu.make_async_copy(p2_hbm, p2, ld.at[0])
    cp_p1 = pltpu.make_async_copy(p1_hbm, p1, ld.at[1])
    cp_x = pltpu.make_async_copy(x_hbm, xv, ld.at[2])
    small = [
        pltpu.make_async_copy(src, dst, ld.at[3 + i])
        for i, (src, dst) in enumerate(
            (
                (w2_hbm, w2), (ct_hbm, ct), (lab_hbm, lab), (m2_hbm, m2), (v2_hbm, v2),
                (w1_hbm, w1), (m1_hbm, m1), (v1_hbm, v1),
            )
        )
    ]
    for copy in small[:3]:
        copy.start()
    cp_p2.start()
    cp_p1.start()
    cp_x.start()
    for copy in small[3:]:
        copy.start()

    bar = pltpu.get_barrier_semaphore()

    def sig_zc(i):
        k = (z * 2 + c + i) % 16
        pl.semaphore_signal(bar, inc=1, device_id=dev(k // 2, x, y, k % 2), device_id_type=MESH)

    def sig_xy(i):
        k = (x * 4 + y + i) % 16
        pl.semaphore_signal(bar, inc=1, device_id=dev(z, k // 4, k % 4, c), device_id_type=MESH)

    loop(1, 16, sig_zc)
    loop(1, 16, sig_xy)

    for copy in small[:3]:
        copy.wait()
    for h in (0, 1):
        wsend[h, 0:9, :] = w2[pl.ds(h, 9, stride=2), :].astype(BF)

    table = jnp.concatenate([ct[...].astype(F32), jnp.zeros((5, CH), F32)], axis=0)
    c3[...] = jnp.concatenate([table] * 4, axis=0).astype(BF)

    slot = z * 2 + c
    place = x * 4 + y

    def g0_copy(i):
        k = (slot + i) % 16
        return rcopy(
            wsend.at[k % 2], g0.at[slot], s_g0.at[i], r_g0.at[slot], dev(k // 2, x, y, k % 2)
        )

    def g0_start():
        g0[slot] = wsend[c]
        loop(1, 16, lambda i: g0_copy(i).start())

    def g1_copy(i):
        return rcopy(
            ga_.at[a, b], ga_.at[a, b], s_g1.at[i], r_g1.at[b], ab(a, (b + i) % NA)
        )

    def g2_copy(k, i):
        return rcopy(
            ga_.at[a, k], ga_.at[a, k], s_g2.at[k, i], r_g2.at[a, k], ab((a + i) % NA, b)
        )

    def g0_finish():
        def one(i):
            k = (slot + i) % 16
            rcopy(g0.at[k], g0.at[k], s_g0.at[i], r_g0.at[k], dev(z, x, y, c)).wait_recv()

        loop(1, 16, one)
        pack = jnp.concatenate([g0[s, 0:16, :].astype(F32)[0:9] for s in range(16)], axis=0)
        ga_[a, b] = pack.astype(BF)
        loop(1, NA, lambda i: g1_copy(i).start())
        loop(1, NA, lambda i: g2_copy(b, i).start())

    def g1_finish():
        for j in (1, 3, 2):
            k = (b + j) % NA
            rcopy(ga_.at[a, k], ga_.at[a, k], s_g1.at[j], r_g1.at[k], ab(a, k)).wait_recv()
            loop(1, NA, lambda i, k=k: g2_copy(k, i).start())

    other = dev(z, x, y, 1 - c)

    def g3_copy():
        return rcopy(wd.at[c], wd.at[c], s_g3, r_g3, other)

    def g2_finish():
        def wait(i):
            k = (a + i) % NA
            for j in range(NA):
                rcopy(
                    ga_.at[k, j], ga_.at[k, j], s_g2.at[j, i], r_g2.at[k, j], ab(k, b)
                ).wait_recv()

        loop(1, NA, wait)

        def unpack(xx):
            base = pl.multiple_of(xx * 72, 8)
            for yy in range(NA):
                block = ga_[(1 - c) * xx + c * yy, (1 - c) * yy + c * xx].astype(F32)
                for zz in range(NZ):
                    wf[pl.ds(base + 288 * zz + 18 * yy, 18), :] = block[18 * zz:18 * zz + 18]

        loop(0, NA, unpack)
        wd[c] = wf[...].astype(BF)
        g3_copy().start()

    cols = lax.broadcasted_iota(jnp.int32, (WD, CH), 0)

    def put_row(layer, row, g):
        at = pl.ds(pl.multiple_of(row * WD, 32), WD)
        gs[layer, 1, at, :] = g.astype(BF)
        gs[layer, 0, at, :] = jnp.where(cols == WD - 1, 0.0, pltpu.roll(g, WD - 1, 0)).astype(BF)
        gs[layer, 2, at, :] = jnp.where(cols == 0, 0.0, pltpu.roll(g, 1, 0)).astype(BF)

    def halo_copy(layer, down):
        src = H if down else 1
        dst = 0 if down else H + 1
        k = 1 if down else 0
        where = dev((z + 1) % NZ, x, y, c) if down else dev((z + NZ - 1) % NZ, x, y, c)
        return rcopy(
            gs.at[layer, 1, pl.ds(src * WD, WD)],
            gs.at[layer, 1, pl.ds(dst * WD, WD)],
            s_h.at[layer, k], r_h.at[layer, k], where,
        )

    def halo_start(layer):
        halo_copy(layer, True).start()
        halo_copy(layer, False).start()

    def halo_finish(layer):
        halo_copy(layer, True).wait_recv()
        halo_copy(layer, False).wait_recv()
        for row, edge in ((0, z == 0), (H + 1, z == NZ - 1)):
            g = gs[layer, 1, pl.ds(row * WD, WD), :].astype(F32)
            put_row(layer, row, jnp.where(edge, 0.0, g))

    cls_row = lax.broadcasted_iota(jnp.int32, (8, WD), 0)
    valid = cls_row < 3

    def second_row(r):
        at = pl.ds(pl.multiple_of(r * WD, 32), WD)
        pre = p2[at, :]
        act = jnp.maximum(pre, jnp.zeros_like(pre))
        logits = lax.dot_general(
            c3[0:16, :], act, (((1,), (1,)), ((), ())), preferred_element_type=F32
        )[0:8]
        top = jnp.max(jnp.where(valid, logits, -1e30), axis=0, keepdims=True)
        expo = jnp.where(valid, jnp.exp(logits - top), 0.0)
        prob = expo / jnp.sum(expo, axis=0, keepdims=True)
        onehot = (cls_row == lab[pl.ds(r, 1), :]).astype(F32)
        dlogit = jnp.where(valid, prob - onehot, 0.0)
        high = dlogit.astype(BF).astype(F32)
        rest = dlogit - high
        mid = rest.astype(BF).astype(F32)
        low = rest - mid
        parts = jnp.concatenate([high, mid, low, jnp.zeros_like(low)], axis=0).astype(BF)
        grad = lax.dot_general(
            parts, c3[...], (((0,), (0,)), ((), ())), preferred_element_type=F32
        )
        put_row(0, r + 1, jnp.where(pre.astype(F32) > 0, grad, 0.0))

    def transpose_in(src, relu):
        def one(k):
            at = pl.ds(pl.multiple_of(k * 256, 256), 256)
            block = src[at, :]
            if relu:
                block = jnp.maximum(block, jnp.zeros_like(block))
            xt[:, at] = block.T

        loop(0, PIX // 256, one)

    def pair_copy(layer, group):
        dy = GROUPS[group]
        rows = pl.ds(dy * 768, 768)
        return rcopy(
            st.at[layer, 1 - c, rows], precv.at[layer, rows],
            s_p.at[layer, group], r_p.at[layer, group], other,
        )

    def taps(layer, group):
        dy = GROUPS[group]

        def one(dx):
            window = gs[layer, dx, pl.ds((2 - dy) * WD, PIX), :]
            part = lax.dot_general(
                xt[...], window, (((1,), (0,)), ((), ())), preferred_element_type=F32
            )
            at = pl.ds((dy * 3 + dx) * 256, 256)
            st[layer, 0, at, :] = part[:, 0:128]
            st[layer, 1, at, :] = part[:, 128:256]

        for dx in range(3):
            one(dx)
        pair_copy(layer, group).start()

    def spans(layer):
        return ((0, 144),) if layer == 0 else tuple(p[:2] for p in PARTS)

    def a_copy(layer, part, i):
        lo, hi = spans(layer)[part]
        k = (place + i) % 16
        return rcopy(
            asend.at[layer, k, pl.ds(lo, hi - lo)], arecv.at[layer, place, pl.ds(lo, hi - lo)],
            s_a.at[layer, part, i], r_a.at[layer, part, place], dev(z, k // 4, k % 4, c),
        )

    def a_sum(layer, group):
        pair_copy(layer, group).wait_recv()
        lo, hi = PARTS[group][3]
        tot[lo:hi, :] = st[layer, c, lo:hi, :] + precv[layer, lo:hi, :]

    def a_start(layer, part):
        lo, hi = spans(layer)[part]

        def one(xx):
            base = pl.multiple_of(xx * 72, 8)
            for yy in range(NA):
                block = jnp.concatenate(
                    [
                        tot[pl.ds(base + 288 * zz + 18 * yy + r, n), :]
                        for zz, r, n in pieces(lo, hi)
                    ],
                    axis=0,
                )
                asend[layer, xx * 4 + yy, lo:hi, :] = block.astype(BF)

        loop(0, NA, one)
        loop(1, 16, lambda i: a_copy(layer, part, i).start())

    def z_copy(layer, k):
        return rcopy(
            zsend.at[layer, k], zrecv.at[layer, slot],
            s_z.at[layer, k], r_z.at[layer, slot], dev(k // 2, x, y, k % 2),
        )

    def a_finish(layer, part, blocks):
        lo, hi = spans(layer)[part]
        rows = pl.ds(lo, hi - lo)

        def wait(i):
            k = (place + i) % 16
            ref = arecv.at[layer, k, rows]
            rcopy(ref, ref, s_a.at[layer, part, i], r_a.at[layer, part, k], other).wait_recv()

        loop(1, 16, wait)
        asum[rows, :] = lax.fori_loop(
            1, 16,
            lambda i, acc: acc + arecv[layer, (place + i) % 16, rows, :].astype(F32),
            asend[layer, place, rows, :].astype(F32),
        )
        for j in blocks:
            for cc in range(2):
                k = 2 * ZORDER[j] + cc
                r = 18 * j + 9 * cc
                zsend[layer, k, 0:9, :] = asum[r:r + 9, :]

                @pl.when(k == slot)
                def _(k=k):
                    zrecv[layer, slot] = zsend[layer, k]

                @pl.when(k != slot)
                def _(k=k):
                    z_copy(layer, k).start()

    def z_finish(layer):
        def wait(i):
            k = (slot + i) % 16
            rcopy(
                zrecv.at[layer, k], zrecv.at[layer, k],
                s_z.at[layer, k], r_z.at[layer, k], other,
            ).wait_recv()

        loop(1, 16, wait)
        for cc in range(2):
            total = zrecv[layer, cc, 0:9, :]
            for zz in range(1, NZ):
                total = total + zrecv[layer, 2 * zz + cc, 0:9, :]
            gfin[layer, pl.ds(cc, 9, stride=2), :] = total
        return gfin[layer]

    def moments(grad, weight, first, second):
        first_new = beta_one * first + (1.0 - beta_one) * grad
        second_new = beta_two * second + (1.0 - beta_two) * grad * grad
        corr_one = 1.0 - beta_one**STEP
        corr_two = 1.0 - beta_two**STEP
        update = (
            first_new / corr_one / (jnp.sqrt(second_new / corr_two) + epsilon)
            + weight_decay * weight
        )
        return (first_new, second_new, update)

    def first_rows(r, n):
        total = jnp.zeros((n * WD, CH), F32)
        for dy in range(3):
            at = pl.ds(pl.multiple_of((r + 2 - dy) * WD, 32), n * WD)
            for dx in range(3):
                t = (dy * 3 + dx) * 256
                tap = jnp.concatenate([wd[0, t:t + 256, :], wd[1, t:t + 256, :]], axis=1)
                total = total + lax.dot_general(
                    gs[0, dx, at, :], tap, (((1,), (1,)), ((), ())), preferred_element_type=F32
                )
        for j in range(n):
            pre = p1[pl.ds(pl.multiple_of((r + j) * WD, 32), WD), :]
            part = total[j * WD:(j + 1) * WD]
            put_row(1, r + j + 1, jnp.where(pre.astype(F32) > 0, part, 0.0))

    cp_p2.wait()
    loop(0, 2, lambda i: second_row(i * (H - 1)))
    pl.semaphore_wait(bar, 30)
    g0_start()
    halo_start(0)
    loop(1, H - 1, second_row)
    g0_finish()
    cp_p1.wait()
    transpose_in(p1, True)
    taps(0, 0)
    g1_finish()
    halo_finish(0)
    taps(0, 1)
    taps(0, 2)
    cp_x.wait()
    transpose_in(xv, False)
    for copy in small[3:]:
        copy.wait()
    g2_finish()
    for group in range(3):
        a_sum(0, group)
    a_start(0, 0)
    g3_copy().wait_recv()
    loop(0, 2, lambda i: first_rows(i * (H - 1), 1))
    halo_start(1)
    loop(0, 2, lambda i: first_rows(1 + 3 * i, 3))
    taps(1, 0)
    halo_finish(1)
    taps(1, 1)
    a_sum(1, 0)
    a_start(1, 0)
    taps(1, 2)
    a_sum(1, 1)
    a_start(1, 1)
    a_sum(1, 2)
    a_start(1, 2)
    a_finish(0, 0, range(NZ))
    a_finish(1, 0, ())
    a_finish(1, 1, range(4))
    a_finish(1, 2, range(4, NZ))
    m2n, v2n, u2 = moments(z_finish(0), w2[...], m2[...], v2[...])
    outs[4, 0:18, :] = m2n
    outs[5, 0:18, :] = v2n
    outs[7, 0:18, :] = u2
    m1n, v1n, u1 = moments(z_finish(1), w1[...], m1[...], v1[...])
    outs[1, 0:18, :] = m1n
    outs[2, 0:18, :] = v1n

    def squares(value):
        return jnp.sum(value * value, axis=0, keepdims=True)

    u2 = outs[7, 0:18, :]
    nbuf[0, slot] = jnp.concatenate(
        [squares(w1[...]), squares(u1), squares(w2[...]), squares(u2), jnp.zeros((4, 128), F32)],
        axis=0,
    )
    def n_copy(stage, i):
        if stage == 0:
            k = (slot + i) % 16
            return rcopy(
                nbuf.at[0, slot], nbuf.at[0, slot], s_n.at[0, i], r_n.at[0, slot],
                dev(k // 2, x, y, k % 2),
            )
        k = (place + i) % 16
        return rcopy(
            nbuf.at[1, place], nbuf.at[1, place], s_n.at[1, i], r_n.at[1, place],
            dev(z, k // 4, k % 4, c),
        )

    def n_wait(stage, i):
        k = ((slot if stage == 0 else place) + i) % 16
        ref = nbuf.at[stage, k]
        rcopy(ref, ref, s_n.at[stage, i], r_n.at[stage, k], other).wait_recv()

    loop(1, 16, lambda i: n_copy(0, i).start())
    loop(1, 16, lambda i: n_wait(0, i))
    nbuf[1, place] = jnp.sum(nbuf[0], axis=0)
    loop(1, 16, lambda i: n_copy(1, i).start())
    loop(1, 16, lambda i: n_wait(1, i))
    sums = jnp.sqrt(jnp.sum(jnp.sum(nbuf[1], axis=0), axis=1, keepdims=True))
    step1 = sums[0:1] / sums[1:2] * u1
    step2 = sums[2:3] / sums[3:4] * u2
    outs[6, 0:18, :] = step1
    outs[7, 0:18, :] = step2
    outs[0, 0:18, :] = w1[...] - learn_rate * step1
    outs[3, 0:18, :] = w2[...] - learn_rate * step2

    def done(i):
        g0_copy(i).wait_send()
        for layer in range(2):
            for part in range(len(spans(layer))):
                a_copy(layer, part, i).wait_send()
            z_copy(layer, (slot + i) % 16).wait_send()
        for stage in range(2):
            n_copy(stage, i).wait_send()

    loop(1, 16, done)

    def done_gather(i):
        g1_copy(i).wait_send()
        for k in range(NA):
            g2_copy(k, i).wait_send()

    loop(1, NA, done_gather)
    g3_copy().wait_send()
    for layer in range(2):
        halo_copy(layer, True).wait_send()
        halo_copy(layer, False).wait_send()
        for group in range(3):
            pair_copy(layer, group).wait_send()


def body(
    inputs, pre_first, pre_second, labels, classifier,
    w_first, m_first, v_first, w_second, m_second, v_second,
):
    flat = [t.reshape(18, 128) for t in (w_first, m_first, v_first, w_second, m_second, v_second)]
    vm = pl.BlockSpec(memory_space=pltpu.VMEM)
    hb = pl.BlockSpec(memory_space=pl.ANY)
    dma = pltpu.SemaphoreType.DMA
    outs = pl.pallas_call(
        kernel,
        out_shape=jax.ShapeDtypeStruct((8, 24, 128), F32),
        in_specs=[hb] * 11,
        out_specs=vm,
        scratch_shapes=[
            pltpu.VMEM((H, WD), jnp.int32),
            pltpu.VMEM((3, CH), BF),
            pltpu.VMEM((18, 128), F32),
            pltpu.VMEM((18, 128), F32),
            pltpu.VMEM((18, 128), F32),
            pltpu.VMEM((18, 128), F32),
            pltpu.VMEM((18, 128), F32),
            pltpu.VMEM((18, 128), F32),
            pltpu.VMEM((PIX, CH), BF),
            pltpu.VMEM((PIX, CH), BF),
            pltpu.VMEM((PIX, CH), BF),
            pltpu.VMEM((CH, PIX), BF),
            pltpu.VMEM((2, 3, (H + 2) * WD, CH), BF),
            pltpu.VMEM((32, CH), BF),
            pltpu.VMEM((2, 16, 128), BF),
            pltpu.VMEM((16, 16, 128), BF),
            pltpu.VMEM((NA, NA, 144, 128), BF),
            pltpu.VMEM((2304, 128), F32),
            pltpu.VMEM((2, 2304, 128), BF),
            pltpu.VMEM((2, 2, 2304, 128), F32),
            pltpu.VMEM((2, 2304, 128), F32),
            pltpu.VMEM((2304, 128), F32),
            pltpu.VMEM((2, 16, 144, 128), BF),
            pltpu.VMEM((2, 16, 144, 128), BF),
            pltpu.VMEM((144, 128), F32),
            pltpu.VMEM((2, 16, 16, 128), F32),
            pltpu.VMEM((2, 16, 16, 128), F32),
            pltpu.VMEM((2, 18, 128), F32),
            pltpu.VMEM((2, 16, 8, 128), F32),
            dma((11,)),
            dma((16,)), dma((16,)),
            dma((NA,)), dma((NA,)),
            dma((NA, NA)), dma((NA, NA)),
            dma, dma,
            dma((2, 2)), dma((2, 2)),
            dma((2, 3)), dma((2, 3)),
            dma((2, 3, 16)), dma((2, 3, 16)),
            dma((2, 16)), dma((2, 16)),
            dma((2, 16)), dma((2, 16)),
        ],
        compiler_params=pltpu.CompilerParams(
            collective_id=0, has_side_effects=True, vmem_limit_bytes=56 * 1024 * 1024
        ),
        cost_estimate=pl.CostEstimate(
            flops=2 * 27 * PIX * CH * CH, bytes_accessed=4_000_000, transcendentals=3 * PIX
        ),
    )(
        inputs.reshape(PIX, CH), pre_first.reshape(PIX, CH), pre_second.reshape(PIX, CH),
        labels[0], classifier.T, *flat,
    )
    return tuple(outs[i, 0:18].reshape(2304) for i in range(8))


def solution(mesh):
    grid = P("dp", "tile", None, None)
    flat = P(("tile", "dp"))
    return jax.shard_map(
        body,
        mesh=mesh,
        in_specs=(grid, grid, grid, P("dp", "tile", None), P(), flat, flat, flat, flat, flat, flat),
        out_specs=(flat,) * 8,
        check_vma=False,
    )
```

```python
import jax
import jax.numpy as jnp
from jax import lax
from jax.experimental import pallas as pl
from jax.experimental.pallas import tpu as pltpu
from jax.sharding import PartitionSpec as P

STEP = 10

beta_one = 0.9
beta_two = 0.999
epsilon = 1e-06
weight_decay = 0.01
learn_rate = 0.002

MESH = pl.DeviceIdType.MESH
BF = jnp.bfloat16
F32 = jnp.float32
NZ, NA = 8, 4
H, WD, CH = 8, 288, 256
PIX = H * WD
GROUPS = (1, 0, 2)
ZORDER = (3, 4, 0, 1, 2, 5, 6, 7)
PARTS = ((0, 32, 0, (768, 1536)), (32, 80, 1, (0, 768)), (80, 144, 2, (1536, 2304)))


def pieces(lo, hi):
    cut = []
    for j, zz in enumerate(ZORDER):
        first, last = max(lo, 18 * j), min(hi, 18 * j + 18)
        if first < last:
            cut.append((zz, first - 18 * j, last - first))
    return cut


def dev(z, x, y, c):
    return {"tile": z, "dp": x * 8 + y * 2 + c}


def rcopy(src, dst, ssem, rsem, where):
    return pltpu.make_async_remote_copy(
        src_ref=src,
        dst_ref=dst,
        send_sem=ssem,
        recv_sem=rsem,
        device_id=where,
        device_id_type=MESH,
    )


def loop(lo, hi, fn):
    lax.fori_loop(lo, hi, lambda i, carry: (fn(i), carry)[1], 0)


def each(lo, hi, fn):
    for i in range(lo, hi):
        fn(i)


def kernel(
    x_hbm, p1_hbm, p2_hbm, lab_hbm, ct_hbm, w1_hbm, m1_hbm, v1_hbm, w2_hbm, m2_hbm, v2_hbm,
    outs,
    lab, ct, w1, m1, v1, w2, m2, v2, xv, p1, p2, xt, gs, c3, wsend, g0, ga_, gb_, wf, wd,
    st, precv, tot, asend, arecv, asum, zsend, zrecv, gfin, nbuf,
    ld, s_g0, r_g0, s_g1, r_g1, s_g2, r_g2, s_g3, r_g3, s_h, r_h,
    s_p, r_p, s_a, r_a, s_z, r_z, s_n, r_n,
):
    z = lax.axis_index("tile")
    d = lax.axis_index("dp")
    x = d // 8
    y = (d // 2) % 4
    c = d % 2
    a = (1 - c) * x + c * y
    b = (1 - c) * y + c * x

    def ab(aa, bb):
        return dev(z, (1 - c) * aa + c * bb, (1 - c) * bb + c * aa, c)

    bar = pltpu.get_barrier_semaphore()

    def sig_zc(i):
        k = (z * 2 + c + i) % 16
        pl.semaphore_signal(bar, inc=1, device_id=dev(k // 2, x, y, k % 2), device_id_type=MESH)

    def sig_xy(i):
        k = (x * 4 + y + i) % 16
        pl.semaphore_signal(bar, inc=1, device_id=dev(z, k // 4, k % 4, c), device_id_type=MESH)

    each(1, 16, sig_zc)
    each(1, 16, sig_xy)

    cp_p2 = pltpu.make_async_copy(p2_hbm, p2, ld.at[0])
    cp_p1 = pltpu.make_async_copy(p1_hbm, p1, ld.at[1])
    cp_x = pltpu.make_async_copy(x_hbm, xv, ld.at[2])
    small = [
        pltpu.make_async_copy(src, dst, ld.at[3 + i])
        for i, (src, dst) in enumerate(
            (
                (w2_hbm, w2), (ct_hbm, ct), (lab_hbm, lab), (m2_hbm, m2), (v2_hbm, v2),
                (w1_hbm, w1), (m1_hbm, m1), (v1_hbm, v1),
            )
        )
    ]
    for copy in small[:3]:
        copy.start()
    cp_p2.start()
    cp_p1.start()
    cp_x.start()
    for copy in small[3:]:
        copy.start()

    for copy in small[:3]:
        copy.wait()
    for h in (0, 1):
        wsend[h, 0:9, :] = w2[pl.ds(h, 9, stride=2), :].astype(BF)

    table = jnp.concatenate([ct[...].astype(F32), jnp.zeros((5, CH), F32)], axis=0)
    c3[...] = jnp.concatenate([table] * 4, axis=0).astype(BF)

    slot = z * 2 + c
    place = x * 4 + y

    def g0_copy(i):
        k = (slot + i) % 16
        return rcopy(
            wsend.at[k % 2], g0.at[slot], s_g0.at[i], r_g0.at[slot], dev(k // 2, x, y, k % 2)
        )

    def g0_start():
        g0[slot] = wsend[c]
        each(1, 16, lambda i: g0_copy(i).start())

    other = dev(z, x, y, 1 - c)

    def g3_copy(j, k):
        return rcopy(ga_.at[j, k], gb_.at[j, k], s_g3.at[j, k], r_g3.at[j, k], other)

    def g1_copy(i):
        return rcopy(
            ga_.at[a, b], ga_.at[a, b], s_g1.at[i], r_g1.at[b], ab(a, (b + i) % NA)
        )

    def g2_copy(k, i):
        return rcopy(
            ga_.at[a, k], ga_.at[a, k], s_g2.at[k, i], r_g2.at[a, k], ab((a + i) % NA, b)
        )

    def g0_finish():
        def one(i):
            k = (slot + i) % 16
            rcopy(g0.at[k], g0.at[k], s_g0.at[i], r_g0.at[k], dev(z, x, y, c)).wait_recv()

        each(1, 16, one)
        pack = jnp.concatenate([g0[s, 0:16, :].astype(F32)[0:9] for s in range(16)], axis=0)
        ga_[a, b] = pack.astype(BF)
        each(1, NA, lambda i: g1_copy(i).start())
        each(1, NA, lambda i: g2_copy(b, i).start())
        g3_copy(a, b).start()

    def g1_finish():
        for j in (1, 3, 2):
            k = (b + j) % NA
            rcopy(ga_.at[a, k], ga_.at[a, k], s_g1.at[j], r_g1.at[k], ab(a, k)).wait_recv()
            each(1, NA, lambda i, k=k: g2_copy(k, i).start())
            g3_copy(a, k).start()

    def unpack(pieces_of, core, half):
        def one(xx):
            base = pl.multiple_of(xx * 72, 8)
            for yy in range(NA):
                block = pieces_of[
                    (1 - core) * xx + core * yy, (1 - core) * yy + core * xx
                ].astype(F32)
                for zz in range(NZ):
                    wf[pl.ds(base + 288 * zz + 18 * yy, 18), :] = block[18 * zz:18 * zz + 18]

        loop(0, NA, one)
        wd[half] = wf[...].astype(BF)

    def g2_finish():
        for i in (1, 3, 2):
            k = (a + i) % NA
            for j in range(NA):
                rcopy(
                    ga_.at[k, j], ga_.at[k, j], s_g2.at[j, i], r_g2.at[k, j], other
                ).wait_recv()
                g3_copy(k, j).start()
        unpack(ga_, c, c)

    def g3_finish():
        for j in range(NA):
            for k in range(NA):
                g3_copy(j, k).wait_recv()
        unpack(gb_, 1 - c, 1 - c)

    cols = lax.broadcasted_iota(jnp.int32, (WD, CH), 0)

    def put_row(layer, row, g):
        at = pl.ds(pl.multiple_of(row * WD, 32), WD)
        gs[layer, 1, at, :] = g.astype(BF)
        gs[layer, 0, at, :] = jnp.where(cols == WD - 1, 0.0, pltpu.roll(g, WD - 1, 0)).astype(BF)
        gs[layer, 2, at, :] = jnp.where(cols == 0, 0.0, pltpu.roll(g, 1, 0)).astype(BF)

    def halo_copy(layer, down):
        src = H if down else 1
        dst = 0 if down else H + 1
        k = 1 if down else 0
        where = dev((z + 1) % NZ, x, y, c) if down else dev((z + NZ - 1) % NZ, x, y, c)
        return rcopy(
            gs.at[layer, 1, pl.ds(src * WD, WD)],
            gs.at[layer, 1, pl.ds(dst * WD, WD)],
            s_h.at[layer, k], r_h.at[layer, k], where,
        )

    def halo_start(layer):
        halo_copy(layer, True).start()
        halo_copy(layer, False).start()

    def halo_finish(layer):
        halo_copy(layer, True).wait_recv()
        halo_copy(layer, False).wait_recv()
        for row, edge in ((0, z == 0), (H + 1, z == NZ - 1)):
            g = gs[layer, 1, pl.ds(row * WD, WD), :].astype(F32)
            put_row(layer, row, jnp.where(edge, 0.0, g))

    cls_row = lax.broadcasted_iota(jnp.int32, (8, WD), 0)
    valid = cls_row < 3

    def second_row(r):
        at = pl.ds(pl.multiple_of(r * WD, 32), WD)
        pre = p2[at, :]
        act = jnp.maximum(pre, jnp.zeros_like(pre))
        logits = lax.dot_general(
            c3[0:16, :], act, (((1,), (1,)), ((), ())), preferred_element_type=F32
        )[0:8]
        top = jnp.max(jnp.where(valid, logits, -1e30), axis=0, keepdims=True)
        expo = jnp.where(valid, jnp.exp(logits - top), 0.0)
        prob = expo / jnp.sum(expo, axis=0, keepdims=True)
        onehot = (cls_row == lab[pl.ds(r, 1), :]).astype(F32)
        dlogit = jnp.where(valid, prob - onehot, 0.0)
        high = dlogit.astype(BF).astype(F32)
        rest = dlogit - high
        mid = rest.astype(BF).astype(F32)
        low = rest - mid
        parts = jnp.concatenate([high, mid, low, jnp.zeros_like(low)], axis=0).astype(BF)
        grad = lax.dot_general(
            parts, c3[...], (((0,), (0,)), ((), ())), preferred_element_type=F32
        )
        put_row(0, r + 1, jnp.where(pre.astype(F32) > 0, grad, 0.0))

    def transpose_in(src, relu):
        def one(k):
            at = pl.ds(pl.multiple_of(k * 256, 256), 256)
            block = src[at, :]
            if relu:
                block = jnp.maximum(block, jnp.zeros_like(block))
            xt[:, at] = block.T

        loop(0, PIX // 256, one)

    def pair_copy(layer, group):
        dy = GROUPS[group]
        rows = pl.ds(dy * 768, 768)
        return rcopy(
            st.at[layer, 1 - c, rows], precv.at[layer, rows],
            s_p.at[layer, group], r_p.at[layer, group], other,
        )

    def taps(layer, group):
        dy = GROUPS[group]

        def one(dx):
            window = gs[layer, dx, pl.ds((2 - dy) * WD, PIX), :]
            part = lax.dot_general(
                xt[...], window, (((1,), (0,)), ((), ())), preferred_element_type=F32
            )
            at = pl.ds((dy * 3 + dx) * 256, 256)
            st[layer, 0, at, :] = part[:, 0:128]
            st[layer, 1, at, :] = part[:, 128:256]

        for dx in range(3):
            one(dx)
        pair_copy(layer, group).start()

    def spans(layer):
        return ((0, 144),) if layer == 0 else tuple(p[:2] for p in PARTS)

    def a_copy(layer, part, i):
        lo, hi = spans(layer)[part]
        k = (place + i) % 16
        return rcopy(
            asend.at[layer, k, pl.ds(lo, hi - lo)], arecv.at[layer, place, pl.ds(lo, hi - lo)],
            s_a.at[layer, part, i], r_a.at[layer, part, place], dev(z, k // 4, k % 4, c),
        )

    def a_sum(layer, group):
        pair_copy(layer, group).wait_recv()
        lo, hi = PARTS[group][3]
        tot[lo:hi, :] = st[layer, c, lo:hi, :] + precv[layer, lo:hi, :]

    def a_start(layer, part):
        lo, hi = spans(layer)[part]

        def one(xx):
            base = pl.multiple_of(xx * 72, 8)
            for yy in range(NA):
                block = jnp.concatenate(
                    [
                        tot[pl.ds(base + 288 * zz + 18 * yy + r, n), :]
                        for zz, r, n in pieces(lo, hi)
                    ],
                    axis=0,
                )
                asend[layer, xx * 4 + yy, lo:hi, :] = block.astype(BF)

        loop(0, NA, one)
        each(1, 16, lambda i: a_copy(layer, part, i).start())

    def z_copy(layer, k):
        return rcopy(
            zsend.at[layer, k], zrecv.at[layer, slot],
            s_z.at[layer, k], r_z.at[layer, slot], dev(k // 2, x, y, k % 2),
        )

    def a_finish(layer, part, blocks):
        lo, hi = spans(layer)[part]
        rows = pl.ds(lo, hi - lo)

        def wait(i):
            k = (place + i) % 16
            ref = arecv.at[layer, k, rows]
            rcopy(ref, ref, s_a.at[layer, part, i], r_a.at[layer, part, k], other).wait_recv()

        each(1, 16, wait)
        asum[rows, :] = lax.fori_loop(
            1, 16,
            lambda i, acc: acc + arecv[layer, (place + i) % 16, rows, :].astype(F32),
            asend[layer, place, rows, :].astype(F32),
        )
        for j in blocks:
            for cc in range(2):
                k = 2 * ZORDER[j] + cc
                r = 18 * j + 9 * cc
                zsend[layer, k, 0:9, :] = asum[r:r + 9, :]

                @pl.when(k == slot)
                def _(k=k):
                    zrecv[layer, slot] = zsend[layer, k]

                @pl.when(k != slot)
                def _(k=k):
                    z_copy(layer, k).start()

    def z_finish(layer):
        def wait(i):
            k = (slot + i) % 16
            rcopy(
                zrecv.at[layer, k], zrecv.at[layer, k],
                s_z.at[layer, k], r_z.at[layer, k], other,
            ).wait_recv()

        each(1, 16, wait)
        for cc in range(2):
            total = zrecv[layer, cc, 0:9, :]
            for zz in range(1, NZ):
                total = total + zrecv[layer, 2 * zz + cc, 0:9, :]
            gfin[layer, pl.ds(cc, 9, stride=2), :] = total
        return gfin[layer]

    def moments(grad, weight, first, second):
        first_new = beta_one * first + (1.0 - beta_one) * grad
        second_new = beta_two * second + (1.0 - beta_two) * grad * grad
        corr_one = 1.0 - beta_one**STEP
        corr_two = 1.0 - beta_two**STEP
        update = (
            first_new / corr_one / (jnp.sqrt(second_new / corr_two) + epsilon)
            + weight_decay * weight
        )
        return (first_new, second_new, update)

    def first_rows(r, n):
        total = jnp.zeros((n * WD, CH), F32)
        for dy in range(3):
            at = pl.ds(pl.multiple_of((r + 2 - dy) * WD, 32), n * WD)
            for dx in range(3):
                t = (dy * 3 + dx) * 256
                tap = jnp.concatenate([wd[0, t:t + 256, :], wd[1, t:t + 256, :]], axis=1)
                total = total + lax.dot_general(
                    gs[0, dx, at, :], tap, (((1,), (1,)), ((), ())), preferred_element_type=F32
                )
        for j in range(n):
            pre = p1[pl.ds(pl.multiple_of((r + j) * WD, 32), WD), :]
            part = total[j * WD:(j + 1) * WD]
            put_row(1, r + j + 1, jnp.where(pre.astype(F32) > 0, part, 0.0))

    cp_p2.wait()
    loop(0, 2, lambda i: second_row(i * (H - 1)))
    pl.semaphore_wait(bar, 30)
    g0_start()
    halo_start(0)
    loop(1, H - 1, second_row)
    g0_finish()
    cp_p1.wait()
    transpose_in(p1, True)
    taps(0, 0)
    g1_finish()
    halo_finish(0)
    taps(0, 1)
    taps(0, 2)
    cp_x.wait()
    transpose_in(xv, False)
    for copy in small[3:]:
        copy.wait()
    g2_finish()
    for group in range(3):
        a_sum(0, group)
    a_start(0, 0)
    g3_finish()
    loop(0, 2, lambda i: first_rows(i * (H - 1), 1))
    halo_start(1)
    loop(0, 2, lambda i: first_rows(1 + 3 * i, 3))
    taps(1, 0)
    halo_finish(1)
    taps(1, 1)
    a_sum(1, 0)
    a_start(1, 0)
    taps(1, 2)
    a_sum(1, 1)
    a_start(1, 1)
    a_sum(1, 2)
    a_start(1, 2)
    a_finish(0, 0, range(NZ))
    a_finish(1, 0, ())
    a_finish(1, 1, range(4))
    a_finish(1, 2, range(4, NZ))
    m2n, v2n, u2 = moments(z_finish(0), w2[...], m2[...], v2[...])
    outs[4, 0:18, :] = m2n
    outs[5, 0:18, :] = v2n
    outs[7, 0:18, :] = u2
    m1n, v1n, u1 = moments(z_finish(1), w1[...], m1[...], v1[...])
    outs[1, 0:18, :] = m1n
    outs[2, 0:18, :] = v1n

    def squares(value):
        return jnp.sum(value * value, axis=0, keepdims=True)

    u2 = outs[7, 0:18, :]
    nbuf[0, slot] = jnp.concatenate(
        [squares(w1[...]), squares(u1), squares(w2[...]), squares(u2), jnp.zeros((4, 128), F32)],
        axis=0,
    )
    def n_copy(stage, i):
        if stage == 0:
            k = (slot + i) % 16
            return rcopy(
                nbuf.at[0, slot], nbuf.at[0, slot], s_n.at[0, i], r_n.at[0, slot],
                dev(k // 2, x, y, k % 2),
            )
        k = (place + i) % 16
        return rcopy(
            nbuf.at[1, place], nbuf.at[1, place], s_n.at[1, i], r_n.at[1, place],
            dev(z, k // 4, k % 4, c),
        )

    def n_wait(stage, i):
        k = ((slot if stage == 0 else place) + i) % 16
        ref = nbuf.at[stage, k]
        rcopy(ref, ref, s_n.at[stage, i], r_n.at[stage, k], other).wait_recv()

    each(1, 16, lambda i: n_copy(0, i).start())
    each(1, 16, lambda i: n_wait(0, i))
    nbuf[1, place] = jnp.sum(nbuf[0], axis=0)
    each(1, 16, lambda i: n_copy(1, i).start())
    each(1, 16, lambda i: n_wait(1, i))
    sums = jnp.sqrt(jnp.sum(jnp.sum(nbuf[1], axis=0), axis=1, keepdims=True))
    step1 = sums[0:1] / sums[1:2] * u1
    step2 = sums[2:3] / sums[3:4] * u2
    outs[6, 0:18, :] = step1
    outs[7, 0:18, :] = step2
    outs[0, 0:18, :] = w1[...] - learn_rate * step1
    outs[3, 0:18, :] = w2[...] - learn_rate * step2

    def done(i):
        g0_copy(i).wait_send()
        for layer in range(2):
            for part in range(len(spans(layer))):
                a_copy(layer, part, i).wait_send()
            z_copy(layer, (slot + i) % 16).wait_send()
        for stage in range(2):
            n_copy(stage, i).wait_send()

    each(1, 16, done)

    def done_gather(i):
        g1_copy(i).wait_send()
        for k in range(NA):
            g2_copy(k, i).wait_send()

    each(1, NA, done_gather)
    for j in range(NA):
        for k in range(NA):
            g3_copy(j, k).wait_send()
    for layer in range(2):
        halo_copy(layer, True).wait_send()
        halo_copy(layer, False).wait_send()
        for group in range(3):
            pair_copy(layer, group).wait_send()


def body(
    inputs, pre_first, pre_second, labels, classifier,
    w_first, m_first, v_first, w_second, m_second, v_second,
):
    flat = [t.reshape(18, 128) for t in (w_first, m_first, v_first, w_second, m_second, v_second)]
    vm = pl.BlockSpec(memory_space=pltpu.VMEM)
    hb = pl.BlockSpec(memory_space=pl.ANY)
    dma = pltpu.SemaphoreType.DMA
    outs = pl.pallas_call(
        kernel,
        out_shape=jax.ShapeDtypeStruct((8, 24, 128), F32),
        in_specs=[hb] * 11,
        out_specs=vm,
        scratch_shapes=[
            pltpu.VMEM((H, WD), jnp.int32),
            pltpu.VMEM((3, CH), BF),
            pltpu.VMEM((18, 128), F32),
            pltpu.VMEM((18, 128), F32),
            pltpu.VMEM((18, 128), F32),
            pltpu.VMEM((18, 128), F32),
            pltpu.VMEM((18, 128), F32),
            pltpu.VMEM((18, 128), F32),
            pltpu.VMEM((PIX, CH), BF),
            pltpu.VMEM((PIX, CH), BF),
            pltpu.VMEM((PIX, CH), BF),
            pltpu.VMEM((CH, PIX), BF),
            pltpu.VMEM((2, 3, (H + 2) * WD, CH), BF),
            pltpu.VMEM((32, CH), BF),
            pltpu.VMEM((2, 16, 128), BF),
            pltpu.VMEM((16, 16, 128), BF),
            pltpu.VMEM((NA, NA, 144, 128), BF),
            pltpu.VMEM((NA, NA, 144, 128), BF),
            pltpu.VMEM((2304, 128), F32),
            pltpu.VMEM((2, 2304, 128), BF),
            pltpu.VMEM((2, 2, 2304, 128), F32),
            pltpu.VMEM((2, 2304, 128), F32),
            pltpu.VMEM((2304, 128), F32),
            pltpu.VMEM((2, 16, 144, 128), BF),
            pltpu.VMEM((2, 16, 144, 128), BF),
            pltpu.VMEM((144, 128), F32),
            pltpu.VMEM((2, 16, 16, 128), F32),
            pltpu.VMEM((2, 16, 16, 128), F32),
            pltpu.VMEM((2, 18, 128), F32),
            pltpu.VMEM((2, 16, 8, 128), F32),
            dma((11,)),
            dma((16,)), dma((16,)),
            dma((NA,)), dma((NA,)),
            dma((NA, NA)), dma((NA, NA)),
            dma((NA, NA)), dma((NA, NA)),
            dma((2, 2)), dma((2, 2)),
            dma((2, 3)), dma((2, 3)),
            dma((2, 3, 16)), dma((2, 3, 16)),
            dma((2, 16)), dma((2, 16)),
            dma((2, 16)), dma((2, 16)),
        ],
        compiler_params=pltpu.CompilerParams(
            collective_id=0, has_side_effects=True, vmem_limit_bytes=56 * 1024 * 1024
        ),
        cost_estimate=pl.CostEstimate(
            flops=2 * 27 * PIX * CH * CH, bytes_accessed=4_000_000, transcendentals=3 * PIX
        ),
    )(
        inputs.reshape(PIX, CH), pre_first.reshape(PIX, CH), pre_second.reshape(PIX, CH),
        labels[0], classifier.T, *flat,
    )
    return tuple(outs[i, 0:18].reshape(2304) for i in range(8))


def solution(mesh):
    grid = P("dp", "tile", None, None)
    flat = P(("tile", "dp"))
    return jax.shard_map(
        body,
        mesh=mesh,
        in_specs=(grid, grid, grid, P("dp", "tile", None), P(), flat, flat, flat, flat, flat, flat),
        out_specs=(flat,) * 8,
        check_vma=False,
    )
```

```python
import jax
import jax.numpy as jnp
from jax import lax
from jax.experimental import pallas as pl
from jax.experimental.pallas import tpu as pltpu
from jax.sharding import PartitionSpec as P

STEP = 10

beta_one = 0.9
beta_two = 0.999
epsilon = 1e-06
weight_decay = 0.01
learn_rate = 0.002

MESH = pl.DeviceIdType.MESH
BF = jnp.bfloat16
F32 = jnp.float32
NZ, NA = 8, 4
H, WD, CH = 8, 288, 256
PIX = H * WD
GROUPS = (1, 0, 2)
ZORDER = (3, 4, 0, 1, 2, 5, 6, 7)
PARTS = ((0, 32, 0, (768, 1536)), (32, 80, 1, (0, 768)), (80, 144, 2, (1536, 2304)))


def pieces(lo, hi):
    cut = []
    for j, zz in enumerate(ZORDER):
        first, last = max(lo, 18 * j), min(hi, 18 * j + 18)
        if first < last:
            cut.append((zz, first - 18 * j, last - first))
    return cut


def dev(z, x, y, c):
    return {"tile": z, "dp": x * 8 + y * 2 + c}


def rcopy(src, dst, ssem, rsem, where):
    return pltpu.make_async_remote_copy(
        src_ref=src,
        dst_ref=dst,
        send_sem=ssem,
        recv_sem=rsem,
        device_id=where,
        device_id_type=MESH,
    )


def loop(lo, hi, fn):
    lax.fori_loop(lo, hi, lambda i, carry: (fn(i), carry)[1], 0)


def aligned(at, step):
    return at if isinstance(at, int) else pl.multiple_of(at, step)


def each(lo, hi, fn):
    for i in range(lo, hi):
        fn(i)


def kernel(
    x_hbm, p1_hbm, p2_hbm, lab_hbm, ct_hbm, w1_hbm, m1_hbm, v1_hbm, w2_hbm, m2_hbm, v2_hbm,
    outs,
    lab, ct, w1, m1, v1, w2, m2, v2, xv, p1, p2, xt, gs, c3, wsend, g0, ga_, gb_, wf, wd,
    st, precv, tot, asend, arecv, asum, zsend, zrecv, gfin, nbuf,
    ld, s_g0, r_g0, s_g1, r_g1, s_g2, r_g2, s_g3, r_g3, s_h, r_h,
    s_p, r_p, s_a, r_a, s_z, r_z, s_n, r_n,
):
    z = lax.axis_index("tile")
    d = lax.axis_index("dp")
    x = d // 8
    y = (d // 2) % 4
    c = d % 2
    a = (1 - c) * x + c * y
    b = (1 - c) * y + c * x

    def ab(aa, bb):
        return dev(z, (1 - c) * aa + c * bb, (1 - c) * bb + c * aa, c)

    bar = pltpu.get_barrier_semaphore()

    def sig_zc(i):
        k = (z * 2 + c + i) % 16
        pl.semaphore_signal(bar, inc=1, device_id=dev(k // 2, x, y, k % 2), device_id_type=MESH)

    def sig_xy(i):
        k = (x * 4 + y + i) % 16
        pl.semaphore_signal(bar, inc=1, device_id=dev(z, k // 4, k % 4, c), device_id_type=MESH)

    each(1, 16, sig_zc)
    each(1, 16, sig_xy)

    cp_p2 = pltpu.make_async_copy(p2_hbm, p2, ld.at[0])
    cp_p1 = pltpu.make_async_copy(p1_hbm, p1, ld.at[1])
    cp_x = pltpu.make_async_copy(x_hbm, xv, ld.at[2])
    small = [
        pltpu.make_async_copy(src, dst, ld.at[3 + i])
        for i, (src, dst) in enumerate(
            (
                (w2_hbm, w2), (ct_hbm, ct), (lab_hbm, lab), (m2_hbm, m2), (v2_hbm, v2),
                (w1_hbm, w1), (m1_hbm, m1), (v1_hbm, v1),
            )
        )
    ]
    for copy in small[:3]:
        copy.start()
    cp_p2.start()
    cp_p1.start()
    cp_x.start()
    for copy in small[3:]:
        copy.start()

    for copy in small[:3]:
        copy.wait()
    for h in (0, 1):
        wsend[h, 0:9, :] = w2[pl.ds(h, 9, stride=2), :].astype(BF)

    table = jnp.concatenate([ct[...].astype(F32), jnp.zeros((5, CH), F32)], axis=0)
    c3[...] = jnp.concatenate([table] * 4, axis=0).astype(BF)

    slot = z * 2 + c
    place = x * 4 + y

    def g0_copy(i):
        k = (slot + i) % 16
        return rcopy(
            wsend.at[k % 2], g0.at[slot], s_g0.at[i], r_g0.at[slot], dev(k // 2, x, y, k % 2)
        )

    def g0_start():
        g0[slot] = wsend[c]
        each(1, 16, lambda i: g0_copy(i).start())

    other = dev(z, x, y, 1 - c)

    def g3_copy(j, k):
        return rcopy(ga_.at[j, k], gb_.at[j, k], s_g3.at[j, k], r_g3.at[j, k], other)

    def g1_copy(i):
        return rcopy(
            ga_.at[a, b], ga_.at[a, b], s_g1.at[i], r_g1.at[b], ab(a, (b + i) % NA)
        )

    def g2_copy(k, i):
        return rcopy(
            ga_.at[a, k], ga_.at[a, k], s_g2.at[k, i], r_g2.at[a, k], ab((a + i) % NA, b)
        )

    def g0_finish():
        def one(i):
            k = (slot + i) % 16
            rcopy(g0.at[k], g0.at[k], s_g0.at[i], r_g0.at[k], dev(z, x, y, c)).wait_recv()

        each(1, 16, one)
        pack = jnp.concatenate([g0[s, 0:16, :].astype(F32)[0:9] for s in range(16)], axis=0)
        ga_[a, b] = pack.astype(BF)
        each(1, NA, lambda i: g1_copy(i).start())
        each(1, NA, lambda i: g2_copy(b, i).start())
        g3_copy(a, b).start()

    def g1_finish():
        for j in (1, 3, 2):
            k = (b + j) % NA
            rcopy(ga_.at[a, k], ga_.at[a, k], s_g1.at[j], r_g1.at[k], ab(a, k)).wait_recv()
            each(1, NA, lambda i, k=k: g2_copy(k, i).start())
            g3_copy(a, k).start()

    def unpack(pieces_of, core, half):
        def one(xx):
            base = pl.multiple_of(xx * 72, 8)
            for yy in range(NA):
                block = pieces_of[
                    (1 - core) * xx + core * yy, (1 - core) * yy + core * xx
                ].astype(F32)
                for zz in range(NZ):
                    wf[pl.ds(base + 288 * zz + 18 * yy, 18), :] = block[18 * zz:18 * zz + 18]

        loop(0, NA, one)
        wd[half] = wf[...].astype(BF)

    def g2_finish():
        for i in (1, 3, 2):
            k = (a + i) % NA
            for j in range(NA):
                rcopy(
                    ga_.at[k, j], ga_.at[k, j], s_g2.at[j, i], r_g2.at[k, j], other
                ).wait_recv()
                g3_copy(k, j).start()
        unpack(ga_, c, c)

    def g3_finish():
        for j in range(NA):
            for k in range(NA):
                g3_copy(j, k).wait_recv()
        unpack(gb_, 1 - c, 1 - c)

    cols = lax.broadcasted_iota(jnp.int32, (WD, CH), 0)

    def put_row(layer, row, g):
        at = pl.ds(pl.multiple_of(row * WD, 32), WD)
        gs[layer, 1, at, :] = g.astype(BF)
        gs[layer, 0, at, :] = jnp.where(cols == WD - 1, 0.0, pltpu.roll(g, WD - 1, 0)).astype(BF)
        gs[layer, 2, at, :] = jnp.where(cols == 0, 0.0, pltpu.roll(g, 1, 0)).astype(BF)

    def halo_copy(layer, down):
        src = H if down else 1
        dst = 0 if down else H + 1
        k = 1 if down else 0
        where = dev((z + 1) % NZ, x, y, c) if down else dev((z + NZ - 1) % NZ, x, y, c)
        return rcopy(
            gs.at[layer, 1, pl.ds(src * WD, WD)],
            gs.at[layer, 1, pl.ds(dst * WD, WD)],
            s_h.at[layer, k], r_h.at[layer, k], where,
        )

    def halo_start(layer):
        halo_copy(layer, True).start()
        halo_copy(layer, False).start()

    def halo_finish(layer):
        halo_copy(layer, True).wait_recv()
        halo_copy(layer, False).wait_recv()
        for row, edge in ((0, z == 0), (H + 1, z == NZ - 1)):
            g = gs[layer, 1, pl.ds(row * WD, WD), :].astype(F32)
            put_row(layer, row, jnp.where(edge, 0.0, g))

    cls_row = lax.broadcasted_iota(jnp.int32, (8, WD), 0)
    valid = cls_row < 3

    def second_row(r):
        at = pl.ds(pl.multiple_of(r * WD, 32), WD)
        pre = p2[at, :]
        act = jnp.maximum(pre, jnp.zeros_like(pre))
        logits = lax.dot_general(
            c3[0:16, :], act, (((1,), (1,)), ((), ())), preferred_element_type=F32
        )[0:8]
        top = jnp.max(jnp.where(valid, logits, -1e30), axis=0, keepdims=True)
        expo = jnp.where(valid, jnp.exp(logits - top), 0.0)
        prob = expo / jnp.sum(expo, axis=0, keepdims=True)
        onehot = (cls_row == lab[pl.ds(r, 1), :]).astype(F32)
        dlogit = jnp.where(valid, prob - onehot, 0.0)
        high = dlogit.astype(BF).astype(F32)
        rest = dlogit - high
        mid = rest.astype(BF).astype(F32)
        low = rest - mid
        parts = jnp.concatenate([high, mid, low, jnp.zeros_like(low)], axis=0).astype(BF)
        grad = lax.dot_general(
            parts, c3[...], (((0,), (0,)), ((), ())), preferred_element_type=F32
        )
        put_row(0, r + 1, jnp.where(pre.astype(F32) > 0, grad, 0.0))

    def transpose_in(src, relu):
        def one(k):
            at = pl.ds(pl.multiple_of(k * 256, 256), 256)
            block = src[at, :]
            if relu:
                block = jnp.maximum(block, jnp.zeros_like(block))
            xt[:, at] = block.T

        loop(0, PIX // 256, one)

    def pair_copy(layer, group):
        dy = GROUPS[group]
        rows = pl.ds(dy * 768, 768)
        return rcopy(
            st.at[layer, 1 - c, rows], precv.at[layer, rows],
            s_p.at[layer, group], r_p.at[layer, group], other,
        )

    def taps(layer, group):
        dy = GROUPS[group]

        def one(dx):
            window = gs[layer, dx, pl.ds((2 - dy) * WD, PIX), :]
            part = lax.dot_general(
                xt[...], window, (((1,), (0,)), ((), ())), preferred_element_type=F32
            )
            at = pl.ds(aligned((dy * 3 + dx) * 256, 256), 256)
            st[layer, 0, at, :] = part[:, 0:128]
            st[layer, 1, at, :] = part[:, 128:256]

        if layer == 0:
            loop(0, 3, one)
        else:
            each(0, 3, one)
        pair_copy(layer, group).start()

    def spans(layer):
        return ((0, 144),) if layer == 0 else tuple(p[:2] for p in PARTS)

    def a_copy(layer, part, i):
        lo, hi = spans(layer)[part]
        k = (place + i) % 16
        return rcopy(
            asend.at[layer, k, pl.ds(lo, hi - lo)], arecv.at[layer, place, pl.ds(lo, hi - lo)],
            s_a.at[layer, part, i], r_a.at[layer, part, place], dev(z, k // 4, k % 4, c),
        )

    def a_sum(layer, group):
        pair_copy(layer, group).wait_recv()
        lo, hi = PARTS[group][3]
        tot[lo:hi, :] = st[layer, c, lo:hi, :] + precv[layer, lo:hi, :]

    def a_start(layer, part):
        lo, hi = spans(layer)[part]

        def one(xx):
            base = pl.multiple_of(xx * 72, 8)
            for yy in range(NA):
                block = jnp.concatenate(
                    [
                        tot[pl.ds(base + 288 * zz + 18 * yy + r, n), :]
                        for zz, r, n in pieces(lo, hi)
                    ],
                    axis=0,
                )
                asend[layer, xx * 4 + yy, lo:hi, :] = block.astype(BF)

        loop(0, NA, one)
        each(1, 16, lambda i: a_copy(layer, part, i).start())

    def z_copy(layer, k):
        return rcopy(
            zsend.at[layer, k], zrecv.at[layer, slot],
            s_z.at[layer, k], r_z.at[layer, slot], dev(k // 2, x, y, k % 2),
        )

    def a_finish(layer, part, blocks):
        lo, hi = spans(layer)[part]
        rows = pl.ds(lo, hi - lo)

        def wait(i):
            k = (place + i) % 16
            ref = arecv.at[layer, k, rows]
            rcopy(ref, ref, s_a.at[layer, part, i], r_a.at[layer, part, k], other).wait_recv()

        each(1, 16, wait)
        asum[rows, :] = lax.fori_loop(
            1, 16,
            lambda i, acc: acc + arecv[layer, (place + i) % 16, rows, :].astype(F32),
            asend[layer, place, rows, :].astype(F32),
        )
        for j in blocks:
            for cc in range(2):
                k = 2 * ZORDER[j] + cc
                r = 18 * j + 9 * cc
                zsend[layer, k, 0:9, :] = asum[r:r + 9, :]

                @pl.when(k == slot)
                def _(k=k):
                    zrecv[layer, slot] = zsend[layer, k]

                @pl.when(k != slot)
                def _(k=k):
                    z_copy(layer, k).start()

    def z_finish(layer):
        def wait(i):
            k = (slot + i) % 16
            rcopy(
                zrecv.at[layer, k], zrecv.at[layer, k],
                s_z.at[layer, k], r_z.at[layer, k], other,
            ).wait_recv()

        each(1, 16, wait)
        for cc in range(2):
            total = zrecv[layer, cc, 0:9, :]
            for zz in range(1, NZ):
                total = total + zrecv[layer, 2 * zz + cc, 0:9, :]
            gfin[layer, pl.ds(cc, 9, stride=2), :] = total
        return gfin[layer]

    def moments(grad, weight, first, second):
        first_new = beta_one * first + (1.0 - beta_one) * grad
        second_new = beta_two * second + (1.0 - beta_two) * grad * grad
        corr_one = 1.0 - beta_one**STEP
        corr_two = 1.0 - beta_two**STEP
        update = (
            first_new / corr_one / (jnp.sqrt(second_new / corr_two) + epsilon)
            + weight_decay * weight
        )
        return (first_new, second_new, update)

    def first_rows(r, n):
        total = jnp.zeros((n * WD, CH), F32)
        for dy in range(3):
            at = pl.ds(pl.multiple_of((r + 2 - dy) * WD, 32), n * WD)
            for dx in range(3):
                t = (dy * 3 + dx) * 256
                tap = jnp.concatenate([wd[0, t:t + 256, :], wd[1, t:t + 256, :]], axis=1)
                total = total + lax.dot_general(
                    gs[0, dx, at, :], tap, (((1,), (1,)), ((), ())), preferred_element_type=F32
                )
        for j in range(n):
            pre = p1[pl.ds(pl.multiple_of((r + j) * WD, 32), WD), :]
            part = total[j * WD:(j + 1) * WD]
            put_row(1, r + j + 1, jnp.where(pre.astype(F32) > 0, part, 0.0))

    cp_p2.wait()
    loop(0, 2, lambda i: second_row(i * (H - 1)))
    pl.semaphore_wait(bar, 30)
    g0_start()
    halo_start(0)
    loop(1, H - 1, second_row)
    g0_finish()
    cp_p1.wait()
    transpose_in(p1, True)
    taps(0, 0)
    g1_finish()
    halo_finish(0)
    taps(0, 1)
    taps(0, 2)
    cp_x.wait()
    transpose_in(xv, False)
    for copy in small[3:]:
        copy.wait()
    for group in range(3):
        a_sum(0, group)
    a_start(0, 0)
    g2_finish()
    g3_finish()
    loop(0, 2, lambda i: first_rows(i * (H - 1), 1))
    halo_start(1)
    loop(0, 2, lambda i: first_rows(1 + 3 * i, 3))
    taps(1, 0)
    halo_finish(1)
    taps(1, 1)
    a_sum(1, 0)
    a_start(1, 0)
    taps(1, 2)
    a_sum(1, 1)
    a_start(1, 1)
    a_sum(1, 2)
    a_start(1, 2)
    a_finish(0, 0, range(NZ))
    a_finish(1, 0, ())
    a_finish(1, 1, range(4))
    a_finish(1, 2, range(4, NZ))
    m2n, v2n, u2 = moments(z_finish(0), w2[...], m2[...], v2[...])
    outs[4, 0:18, :] = m2n
    outs[5, 0:18, :] = v2n
    outs[7, 0:18, :] = u2
    m1n, v1n, u1 = moments(z_finish(1), w1[...], m1[...], v1[...])
    outs[1, 0:18, :] = m1n
    outs[2, 0:18, :] = v1n

    def squares(value):
        return jnp.sum(value * value, axis=0, keepdims=True)

    u2 = outs[7, 0:18, :]
    nbuf[0, slot] = jnp.concatenate(
        [squares(w1[...]), squares(u1), squares(w2[...]), squares(u2), jnp.zeros((4, 128), F32)],
        axis=0,
    )
    def n_copy(stage, i):
        if stage == 0:
            k = (slot + i) % 16
            return rcopy(
                nbuf.at[0, slot], nbuf.at[0, slot], s_n.at[0, i], r_n.at[0, slot],
                dev(k // 2, x, y, k % 2),
            )
        k = (place + i) % 16
        return rcopy(
            nbuf.at[1, place], nbuf.at[1, place], s_n.at[1, i], r_n.at[1, place],
            dev(z, k // 4, k % 4, c),
        )

    def n_wait(stage, i):
        k = ((slot if stage == 0 else place) + i) % 16
        ref = nbuf.at[stage, k]
        rcopy(ref, ref, s_n.at[stage, i], r_n.at[stage, k], other).wait_recv()

    each(1, 16, lambda i: n_copy(0, i).start())
    each(1, 16, lambda i: n_wait(0, i))
    nbuf[1, place] = jnp.sum(nbuf[0], axis=0)
    each(1, 16, lambda i: n_copy(1, i).start())
    each(1, 16, lambda i: n_wait(1, i))
    sums = jnp.sqrt(jnp.sum(jnp.sum(nbuf[1], axis=0), axis=1, keepdims=True))
    step1 = sums[0:1] / sums[1:2] * u1
    step2 = sums[2:3] / sums[3:4] * u2
    outs[6, 0:18, :] = step1
    outs[7, 0:18, :] = step2
    outs[0, 0:18, :] = w1[...] - learn_rate * step1
    outs[3, 0:18, :] = w2[...] - learn_rate * step2

    def done(i):
        g0_copy(i).wait_send()
        for layer in range(2):
            for part in range(len(spans(layer))):
                a_copy(layer, part, i).wait_send()
            z_copy(layer, (slot + i) % 16).wait_send()
        for stage in range(2):
            n_copy(stage, i).wait_send()

    each(1, 16, done)

    def done_gather(i):
        g1_copy(i).wait_send()
        for k in range(NA):
            g2_copy(k, i).wait_send()

    each(1, NA, done_gather)
    for j in range(NA):
        for k in range(NA):
            g3_copy(j, k).wait_send()
    for layer in range(2):
        halo_copy(layer, True).wait_send()
        halo_copy(layer, False).wait_send()
        for group in range(3):
            pair_copy(layer, group).wait_send()


def body(
    inputs, pre_first, pre_second, labels, classifier,
    w_first, m_first, v_first, w_second, m_second, v_second,
):
    flat = [t.reshape(18, 128) for t in (w_first, m_first, v_first, w_second, m_second, v_second)]
    vm = pl.BlockSpec(memory_space=pltpu.VMEM)
    hb = pl.BlockSpec(memory_space=pl.ANY)
    dma = pltpu.SemaphoreType.DMA
    outs = pl.pallas_call(
        kernel,
        out_shape=jax.ShapeDtypeStruct((8, 24, 128), F32),
        in_specs=[hb] * 11,
        out_specs=vm,
        scratch_shapes=[
            pltpu.VMEM((H, WD), jnp.int32),
            pltpu.VMEM((3, CH), BF),
            pltpu.VMEM((18, 128), F32),
            pltpu.VMEM((18, 128), F32),
            pltpu.VMEM((18, 128), F32),
            pltpu.VMEM((18, 128), F32),
            pltpu.VMEM((18, 128), F32),
            pltpu.VMEM((18, 128), F32),
            pltpu.VMEM((PIX, CH), BF),
            pltpu.VMEM((PIX, CH), BF),
            pltpu.VMEM((PIX, CH), BF),
            pltpu.VMEM((CH, PIX), BF),
            pltpu.VMEM((2, 3, (H + 2) * WD, CH), BF),
            pltpu.VMEM((32, CH), BF),
            pltpu.VMEM((2, 16, 128), BF),
            pltpu.VMEM((16, 16, 128), BF),
            pltpu.VMEM((NA, NA, 144, 128), BF),
            pltpu.VMEM((NA, NA, 144, 128), BF),
            pltpu.VMEM((2304, 128), F32),
            pltpu.VMEM((2, 2304, 128), BF),
            pltpu.VMEM((2, 2, 2304, 128), F32),
            pltpu.VMEM((2, 2304, 128), F32),
            pltpu.VMEM((2304, 128), F32),
            pltpu.VMEM((2, 16, 144, 128), BF),
            pltpu.VMEM((2, 16, 144, 128), BF),
            pltpu.VMEM((144, 128), F32),
            pltpu.VMEM((2, 16, 16, 128), F32),
            pltpu.VMEM((2, 16, 16, 128), F32),
            pltpu.VMEM((2, 18, 128), F32),
            pltpu.VMEM((2, 16, 8, 128), F32),
            dma((11,)),
            dma((16,)), dma((16,)),
            dma((NA,)), dma((NA,)),
            dma((NA, NA)), dma((NA, NA)),
            dma((NA, NA)), dma((NA, NA)),
            dma((2, 2)), dma((2, 2)),
            dma((2, 3)), dma((2, 3)),
            dma((2, 3, 16)), dma((2, 3, 16)),
            dma((2, 16)), dma((2, 16)),
            dma((2, 16)), dma((2, 16)),
        ],
        compiler_params=pltpu.CompilerParams(
            collective_id=0, has_side_effects=True, vmem_limit_bytes=56 * 1024 * 1024
        ),
        cost_estimate=pl.CostEstimate(
            flops=2 * 27 * PIX * CH * CH, bytes_accessed=4_000_000, transcendentals=3 * PIX
        ),
    )(
        inputs.reshape(PIX, CH), pre_first.reshape(PIX, CH), pre_second.reshape(PIX, CH),
        labels[0], classifier.T, *flat,
    )
    return tuple(outs[i, 0:18].reshape(2304) for i in range(8))


def solution(mesh):
    grid = P("dp", "tile", None, None)
    flat = P(("tile", "dp"))
    return jax.shard_map(
        body,
        mesh=mesh,
        in_specs=(grid, grid, grid, P("dp", "tile", None), P(), flat, flat, flat, flat, flat, flat),
        out_specs=(flat,) * 8,
        check_vma=False,
    )
```
